32 devices in a mesh: grp: 2 (over x), seq: 16 (over z, y, core).
Axes of the slice: x: 2, y: 2, z: 4, core: 2. Of those that a mesh axis runs over, the one named last changes fastest.
Arguments:
- activations: bfloat16 [16384, 1536], P(('grp', 'seq')), parts along dimension 0, may hold values from -60 to 60, as said below
- dilated_tap_weight: bfloat16 [3, 1536, 768], replicated, may hold values from -0.09375 to 0.09375
- conv_mix: bfloat16 [768, 1536], replicated, may hold values from -0.21875 to 0.21875
- w_query: bfloat16 [1536, 128], replicated, may hold values from -0.15625 to 0.15625
- w_keyval: bfloat16 [1536, 256], replicated, may hold values from -0.15625 to 0.15625
- contact_tiles: bfloat16 [16, 128, 128], replicated, may hold values from -8 to 250, as said below
- tile_codes: int32 [128, 65], P(('grp', 'seq')), parts along dimension 0, may hold values from 0 to 15
- bin_valid: int32 [16384], P('grp'), parts along dimension 0, may hold values 0 or 1
Outputs:
- attended: bfloat16 [16384, 128], P(('grp', 'seq')), parts along dimension 0
The draws below stay inside these ranges and needn't reach their ends.
There are 2 independent parts, one for each index of `grp`. The reference program is written for one: setup_inputs(seed, part) draws one part's arguments, and reference() takes and returns one part's arrays. A program takes and returns all parts, laid end to end along the dimension named above; an argument that names none is the same for every part. Nothing has to cross between parts.
Inputs may be any that keep to these rules, and one draw needn't show every extreme that they name: `activations`: finite values. `contact_tiles`: finite values.
All inputs are finite; a program needn't handle non-finite values.
Results may differ from the reference program's by a relative error of at most 0.005.
Values may be sent and summed in bfloat16 or wider, within the bound.
A program may use at most 64 MiB of HBM per device.

```python
import math
import jax
import jax.numpy as jnp
from jax import lax

C = 1536
HID = 768
HEADS = 1
HDIM = 128
CONV_DILATION = 8
HALF = 4096
TILE = 128
NCODE = 16
WINDOW_BINS = 8192
NOFF = 65
QTILES = 64


def draw_activations(key, part):
    key_rows = jax.random.fold_in(key, 11)
    key_cols = jax.random.fold_in(key, 12)
    key_base = jax.random.fold_in(key, 13)
    row_scale = jnp.exp(jax.random.uniform(key_rows, (WINDOW_BINS, 1), jnp.float32, math.log(0.3), math.log(3.0)))
    col_scale = jnp.exp(jax.random.uniform(key_cols, (1, C), jnp.float32, math.log(0.3), math.log(3.0)))
    base_draw = jnp.clip(jax.random.normal(key_base, (WINDOW_BINS, C), jnp.float32), -5.0, 5.0)
    return (row_scale * col_scale * base_draw).astype(jnp.bfloat16)


def draw_contact_tiles(key, part):
    key_base = jax.random.fold_in(key, 21)
    result = 2.0 * jnp.clip(jax.random.normal(key_base, (NCODE, TILE, TILE), jnp.float32), -4.0, 4.0)
    return result.astype(jnp.bfloat16)


def touch_ends(entries, rng, low, high):
    place = [jax.random.randint(jax.random.fold_in(rng, axis), (), 0, length) for axis, length in enumerate(entries.shape)]
    longest = entries.shape.index(max(entries.shape))
    neighbour = place[:longest] + [(place[longest] + 1) % entries.shape[longest]] + place[longest + 1:]
    return entries.at[tuple(place)].set(low).at[tuple(neighbour)].set(high)


def normal_values(stream_key, shape, spread, reach, kind=jnp.bfloat16):
    return jnp.clip(spread * jax.random.normal(stream_key, shape, jnp.float32), -reach, reach).astype(kind)


def setup_inputs(seed: int = 0, part: int = 0) -> dict:
    arg_keys = jax.random.split(jax.random.key(seed), 9)
    part_keys = jax.random.split(jax.random.fold_in(arg_keys[8], part), 9)
    activations = draw_activations(jax.random.fold_in(jax.random.fold_in(arg_keys[8], part), 71), part)
    dilated_tap_weight = normal_values(arg_keys[1], (3, C, HID), (3 * C) ** -0.5, 0.09375)
    conv_mix = normal_values(arg_keys[2], (HID, C), HID ** -0.5, 0.21875)
    w_query = normal_values(arg_keys[3], (C, HEADS * HDIM), C ** -0.5, 0.15625)
    w_keyval = normal_values(arg_keys[4], (C, 2 * HEADS * HDIM), C ** -0.5, 0.15625)
    contact_tiles = draw_contact_tiles(jax.random.fold_in(arg_keys[8], 71), part)
    tile_codes = touch_ends(jax.random.randint(part_keys[6], (QTILES, NOFF), 0, NCODE), jax.random.fold_in(part_keys[6], 1), 0, NCODE - 1).astype(jnp.int32)
    bin_valid = touch_ends((jax.random.randint(part_keys[7], (WINDOW_BINS,), 0, 8) < 7).astype(jnp.int32), jax.random.fold_in(part_keys[7], 1), 0, 1)
    return dict(activations=activations, dilated_tap_weight=dilated_tap_weight, conv_mix=conv_mix, w_query=w_query, w_keyval=w_keyval, contact_tiles=contact_tiles, tile_codes=tile_codes, bin_valid=bin_valid)


masked_score = -1e+30
norm_eps = 1e-06

def reference(activations, dilated_tap_weight, conv_mix, w_query, w_keyval, contact_tiles, tile_codes, bin_valid):
    raised_features = jax.nn.gelu(activations.astype(jnp.float32), approximate=False).astype(jnp.bfloat16)
    border_padded = jnp.pad(raised_features, ((CONV_DILATION, CONV_DILATION), (0, 0)))
    conv_sum = jnp.zeros((WINDOW_BINS, HID), jnp.float32)
    for tap_position in range(3):
        offset_features = border_padded[tap_position * CONV_DILATION:tap_position * CONV_DILATION + WINDOW_BINS]
        conv_sum = conv_sum + jnp.dot(offset_features, dilated_tap_weight[tap_position], preferred_element_type=jnp.float32)
    squeezed = jax.nn.gelu(conv_sum, approximate=False).astype(jnp.bfloat16)
    mixed_rows = activations.astype(jnp.float32) + jnp.dot(squeezed, conv_mix, preferred_element_type=jnp.float32)
    normed = (mixed_rows * lax.rsqrt(lax.optimization_barrier(jnp.mean(mixed_rows * mixed_rows, axis=-1, keepdims=True)) + norm_eps)).astype(jnp.bfloat16)
    queries = lax.optimization_barrier(jnp.dot(normed, w_query, preferred_element_type=jnp.float32).astype(jnp.bfloat16))
    keyval = lax.optimization_barrier(jnp.dot(normed, w_keyval, preferred_element_type=jnp.float32).astype(jnp.bfloat16))
    width_heads = HEADS * HDIM
    block_rows = math.gcd(WINDOW_BINS, 512)
    window = block_rows + 2 * HALF
    kv_padded = jnp.pad(keyval, ((HALF, HALF), (0, 0)))
    valid_padded = jnp.pad(bin_valid, (HALF, HALF))
    scale = 1.0 / math.sqrt(HDIM)

    def one_block(block_start):
        query_heads = lax.dynamic_slice(queries, (block_start, jnp.int32(0)), (block_rows, width_heads)).reshape(block_rows, HEADS, HDIM).astype(jnp.float32)
        kv_block = lax.dynamic_slice(kv_padded, (block_start, jnp.int32(0)), (window, 2 * width_heads))
        valid_keys = lax.dynamic_slice_in_dim(valid_padded, block_start, window)
        query_pos = block_start + jnp.arange(block_rows, dtype=jnp.int32)
        key_pos = block_start - HALF + jnp.arange(window, dtype=jnp.int32)
        key_heads = kv_block[:, :width_heads].reshape(window, HEADS, HDIM).astype(jnp.float32)
        value_heads = kv_block[:, width_heads:].reshape(window, HEADS, HDIM).astype(jnp.float32)
        raw_scores = jnp.einsum('qhd,khd->qhk', query_heads, key_heads) * scale
        query_tiles = query_pos // TILE
        key_tiles = jnp.floor_divide(key_pos, TILE)
        offset = jnp.clip(key_tiles[None, :] - query_tiles[:, None] + HALF // TILE, 0, NOFF - 1).astype(jnp.int32)
        picked = tile_codes[query_tiles[:, None], offset]
        bias_block = contact_tiles[picked, (query_pos % TILE)[:, None], jnp.remainder(key_pos, TILE)[None, :]].astype(jnp.float32)
        inside = (key_pos >= 0) & (key_pos < WINDOW_BINS)
        in_band = jnp.abs(key_pos[None, :] - query_pos[:, None]) <= HALF
        kept_pairs = inside[None, :] & in_band & ((valid_keys[None, :] == 1) | (key_pos[None, :] == query_pos[:, None]))
        scores = jnp.where(kept_pairs[:, None, :], raw_scores + bias_block[:, None, :], masked_score)
        row_peak = lax.optimization_barrier(jnp.max(scores, axis=-1, keepdims=True))
        probs = jnp.exp(scores - row_peak)
        row_total = lax.optimization_barrier(jnp.sum(probs, axis=-1))
        rounded = lax.optimization_barrier(probs.astype(jnp.bfloat16)).astype(jnp.float32)
        weighted = jnp.einsum('qhk,khd->qhd', rounded, value_heads)
        return (weighted / row_total[..., None]).reshape(block_rows, width_heads).astype(jnp.bfloat16)
    starts = (jnp.arange(WINDOW_BINS // block_rows, dtype=jnp.int32) * block_rows).astype(jnp.int32)
    blocks = lax.map(one_block, starts)
    return blocks.reshape(WINDOW_BINS, width_heads)
```

```python
import functools
import math

import jax
import jax.numpy as jnp
from jax import lax
from jax.experimental import pallas as pl
from jax.experimental.pallas import tpu as pltpu
from jax.sharding import PartitionSpec as P

HDIM = 128
CONV_DILATION = 8
HALF = 4096
MESH = pl.DeviceIdType.MESH

masked_score = -1e30
norm_eps = 1e-06


def padded(x, axis, width):
    size, length = lax.axis_size(axis), x.shape[0]
    up = [(i, i + 1) for i in range(size - 1)]
    down = [(j, i) for i, j in up]
    before = lax.ppermute(x[length - width :], axis, up)
    after = lax.ppermute(x[:width], axis, down)
    return jnp.concatenate([before, x, after], axis=0)


class Place:
    def __init__(self, count, columns, reach):
        self.count = count
        self.columns = columns
        self.plane = 2 * columns
        self.planes = count // self.plane
        self.reach = reach
        self.far = -(-reach // self.plane)
        self.steps = (2 * self.far + 1) * columns
        me = lax.axis_index("seq")
        self.me = me
        self.z = me // self.plane
        self.y = (me % self.plane) // 2
        self.core = me % 2

    def index(self, z, y, core):
        return z * self.plane + y * 2 + core

    def step(self, k):
        kk = jnp.maximum(k - self.columns, 0)
        rem = kk % (2 * self.columns)
        late = k >= self.columns
        dz = jnp.where(late, (kk // (2 * self.columns) + 1) * (2 * (rem % 2) - 1), 0)
        flip = jnp.where(late, rem // 2, k)
        return dz, flip

    def needs(self, source, target):
        return jnp.abs(source - target) <= self.reach


def block_moves(place, kvbuf, send_sem, recv_sem, dz, flip, half, rows):
    z, y, core = place.z, place.y, place.core
    source_z = z + dz
    source = place.index(source_z, (y + flip) % 2 if place.columns == 2 else y, core)
    held = (source_z >= 0) & (source_z < place.planes) & place.needs(source, place.me)
    piece = kvbuf.at[source, pl.ds(half * rows, rows)]
    slot = (dz + place.far) * place.columns + flip
    edge = (source_z == 0) | (source_z == place.planes - 1)
    away = jnp.abs(dz)

    def along_z(distance):
        return (distance == 1) & (edge | (half == 1))

    def copy(kind, target):
        return pltpu.make_async_remote_copy(
            src_ref=piece,
            dst_ref=piece,
            send_sem=send_sem.at[kind, slot, half],
            recv_sem=recv_sem.at[source, half],
            device_id={"seq": target},
            device_id_type=MESH,
        )

    moves = []
    for kind, turn in ((0, 1), (1, -1)):
        target = jnp.clip(place.index(z + turn, y, core), 0, place.count - 1)
        go = held & (z + turn >= 0) & (z + turn < place.planes)
        go = go & (dz * turn <= 0) & (away + 1 <= place.far) & place.needs(source, target)
        go = go & ((flip == 0) | along_z(away + 1))
        moves.append((go, copy(kind, target)))
    if place.columns == 2:
        target = place.index(z, 1 - y, core)
        go = held & (flip == 0) & ((dz == 0) | jnp.logical_not(along_z(away)))
        moves.append((go & place.needs(source, target), copy(2, target)))
    target = place.index(z, y, 1 - core)
    moves.append((held & place.needs(source, target), copy(3, target)))
    return source, held, moves


def attention_kernel(
    columns,
    count,
    q_ref,
    kv_ref,
    table_ref,
    codes_ref,
    valid_ref,
    out_ref,
    kvbuf,
    peak,
    total,
    weighted,
    send_sem,
    recv_sem,
):
    rows = q_ref.shape[0]
    half_rows = rows // 2
    tile = table_ref.shape[1]
    tiles = rows // tile
    offsets = codes_ref.shape[1]
    place = Place(count, columns, HALF // rows)
    me, z, y, core = place.me, place.z, place.y, place.core
    scale = 1.0 / math.sqrt(HDIM)

    barrier = pltpu.get_barrier_semaphore()
    greeted = [(jnp.bool_(True), place.index(z, y, 1 - core))]
    if columns == 2:
        greeted.append((jnp.bool_(True), place.index(z, 1 - y, core)))
    for turn in (1, -1):
        ok = (z + turn >= 0) & (z + turn < place.planes)
        greeted.append((ok, jnp.clip(place.index(z + turn, y, core), 0, count - 1)))
    for ok, target in greeted:

        @pl.when(ok)
        def _():
            pl.semaphore_signal(barrier, inc=1, device_id={"seq": target}, device_id_type=MESH)

    pl.semaphore_wait(barrier, sum(ok.astype(jnp.int32) for ok, _target in greeted))

    kvbuf[me] = kv_ref[...]
    peak[...] = jnp.full(peak.shape, masked_score, jnp.float32)
    total[...] = jnp.zeros(total.shape, jnp.float32)
    weighted[...] = jnp.zeros(weighted.shape, jnp.float32)

    def absorb(source, special):
        delta = source - me
        keys = kvbuf[source, :, :HDIM]
        values = kvbuf[source, :, HDIM:]
        raw = lax.dot_general(
            q_ref[...], keys, (((1,), (1,)), ((), ())), preferred_element_type=jnp.float32
        )
        bias = []
        for i in range(tiles):
            line = []
            for j in range(tiles):
                offset = jnp.clip(delta * tiles + (j - i) + offsets // 2, 0, offsets - 1)
                line.append(table_ref[codes_ref[i, offset]])
            bias.append(jnp.concatenate(line, axis=1))
        scores = raw * scale + jnp.concatenate(bias, axis=0)
        if special:
            row = lax.broadcasted_iota(jnp.int32, (rows, rows), 0)
            col = lax.broadcasted_iota(jnp.int32, (rows, rows), 1)
            apart = delta * rows + col - row
            kept = (apart == 0) | ((jnp.abs(apart) <= HALF) & (valid_ref[source] >= 0.0))
            scores = jnp.where(kept, scores, masked_score)
        else:
            scores = scores + valid_ref[source]
        old = peak[...]
        new = jnp.maximum(old, jnp.max(scores, axis=1, keepdims=True))
        probs = jnp.exp(scores - new)
        shrink = jnp.exp(old - new)
        peak[...] = new
        total[...] = total[...] * shrink + jnp.sum(probs, axis=1, keepdims=True)
        weighted[...] = weighted[...] * shrink + jnp.dot(
            probs.astype(jnp.bfloat16), values, preferred_element_type=jnp.float32
        )

    def absorb_block(source):
        apart = jnp.abs(source - me)
        special = (apart == 0) | (apart == place.reach)

        @pl.when(special)
        def _():
            absorb(source, True)

        @pl.when(jnp.logical_not(special))
        def _():
            absorb(source, False)

    def arrived(source, half):
        piece = kvbuf.at[source, pl.ds(half * half_rows, half_rows)]
        pltpu.make_async_copy(piece, piece, recv_sem.at[source, half]).wait()

    def moves_of(k, half):
        dz, flip = place.step(k)
        return block_moves(place, kvbuf, send_sem, recv_sem, dz, flip, half, half_rows)

    def turn_of(k, carry):
        for half in range(2):
            source, held, moves = moves_of(k, half)
            held = held & (k < place.steps)

            @pl.when(held & (k > 0))
            def _():
                arrived(source, half)

            for go, copy in moves:

                @pl.when(go & held)
                def _():
                    copy.start()

        dz, flip = place.step(jnp.maximum(k - 1, 0))
        other_z = z + dz
        other = place.index(other_z, (y + flip) % 2 if columns == 2 else y, 1 - core)
        take = (k > 0) & (other_z >= 0) & (other_z < place.planes) & place.needs(other, me)

        @pl.when(held)
        def _():
            absorb_block(source)

        @pl.when(take)
        def _():
            arrived(other, 0)
            arrived(other, 1)
            absorb_block(other)

        return carry

    lax.fori_loop(0, place.steps + 1, turn_of, 0)
    out_ref[...] = (weighted[...] / total[...]).astype(out_ref.dtype)

    def drain(k, carry):
        for half in range(2):
            _source, _held, moves = moves_of(k, half)
            for go, copy in moves:

                @pl.when(go)
                def _():
                    copy.wait_send()

        return carry

    lax.fori_loop(0, place.steps, drain, 0)


def attention(columns, queries, keyval, table, codes, valid):
    rows = queries.shape[0]
    count = lax.axis_size("seq")
    plane = 2 * columns
    far = -(-(HALF // rows) // plane)
    vmem = pl.BlockSpec(memory_space=pltpu.VMEM)
    smem = pl.BlockSpec(memory_space=pltpu.SMEM)
    return pl.pallas_call(
        functools.partial(attention_kernel, columns, count),
        out_shape=jax.ShapeDtypeStruct((rows, HDIM), jnp.bfloat16),
        in_specs=[vmem, vmem, vmem, smem, vmem],
        out_specs=vmem,
        scratch_shapes=[
            pltpu.VMEM((count, rows, 2 * HDIM), jnp.bfloat16),
            pltpu.VMEM((rows, 1), jnp.float32),
            pltpu.VMEM((rows, 1), jnp.float32),
            pltpu.VMEM((rows, HDIM), jnp.float32),
            pltpu.SemaphoreType.DMA((4, (2 * far + 1) * columns, 2)),
            pltpu.SemaphoreType.DMA((count, 2)),
        ],
        compiler_params=pltpu.CompilerParams(
            collective_id=0, has_side_effects=True, vmem_limit_bytes=48 * 1024 * 1024
        ),
        cost_estimate=pl.CostEstimate(
            flops=4 * rows * HDIM * 2 * HALF,
            bytes_accessed=4 * 1024 * 1024,
            transcendentals=rows * 2 * HALF,
        ),
    )(queries, keyval, table, codes, valid)


def per_device(
    columns,
    activations,
    dilated_tap_weight,
    conv_mix,
    w_query,
    w_keyval,
    contact_tiles,
    tile_codes,
    bin_valid,
):
    rows = activations.shape[0]
    count = lax.axis_size("seq")
    border_padded = padded(activations, "seq", CONV_DILATION)
    lifted = jax.nn.gelu(border_padded.astype(jnp.float32), approximate=False).astype(jnp.bfloat16)
    conv_sum = jnp.zeros((rows, dilated_tap_weight.shape[2]), jnp.float32)
    for tap in range(3):
        conv_sum = conv_sum + jnp.dot(
            lifted[tap * CONV_DILATION : tap * CONV_DILATION + rows],
            dilated_tap_weight[tap],
            preferred_element_type=jnp.float32,
        )
    squeezed = jax.nn.gelu(conv_sum, approximate=False).astype(jnp.bfloat16)
    mixed_rows = activations.astype(jnp.float32) + jnp.dot(
        squeezed, conv_mix, preferred_element_type=jnp.float32
    )
    normed = (
        mixed_rows * lax.rsqrt(jnp.mean(mixed_rows * mixed_rows, axis=-1, keepdims=True) + norm_eps)
    ).astype(jnp.bfloat16)
    queries = jnp.dot(normed, w_query, preferred_element_type=jnp.float32).astype(jnp.bfloat16)
    keyval = jnp.dot(normed, w_keyval, preferred_element_type=jnp.float32).astype(jnp.bfloat16)
    valid = jnp.where(bin_valid == 1, 0.0, masked_score).astype(jnp.float32)
    valid = valid.reshape(count, 1, rows)
    table = contact_tiles.astype(jnp.float32)
    return attention(columns, queries, keyval, table, tile_codes, valid)


def columns_of(mesh):
    along = mesh.devices.reshape(-1, mesh.shape["seq"])[0]
    first = along[0]
    if not hasattr(first, "coords"):
        return 2 if mesh.shape["seq"] == 16 else 1
    return sum(d.coords[2] == first.coords[2] for d in along) // 2


def solution(mesh):
    in_specs = (P(("grp", "seq"), None), P(), P(), P(), P(), P(), P(("grp", "seq"), None), P("grp"))
    out_specs = P(("grp", "seq"), None)
    return jax.shard_map(
        functools.partial(per_device, columns_of(mesh)),
        mesh=mesh,
        in_specs=in_specs,
        out_specs=out_specs,
        check_vma=False,
    )
```

```python
import functools
import math

import jax
import jax.numpy as jnp
from jax import lax
from jax.experimental import pallas as pl
from jax.experimental.pallas import tpu as pltpu
from jax.sharding import PartitionSpec as P

HDIM = 128
CONV_DILATION = 8
HALF = 4096
MESH = pl.DeviceIdType.MESH

masked_score = -1e30
norm_eps = 1e-06
LOG2E = math.log2(math.e)


class Place:
    def __init__(self, count, columns, reach):
        self.count = count
        self.columns = columns
        self.plane = 2 * columns
        self.planes = count // self.plane
        self.reach = reach
        self.far = -(-reach // self.plane)
        self.steps = (2 * self.far + 1) * columns
        me = lax.axis_index("seq")
        self.me = me
        self.z = me // self.plane
        self.y = (me % self.plane) // 2
        self.core = me % 2

    def index(self, z, y, core):
        return z * self.plane + y * 2 + core

    def step(self, k):
        kk = jnp.maximum(k - self.columns, 0)
        rem = kk % (2 * self.columns)
        late = k >= self.columns
        dz = jnp.where(late, (kk // (2 * self.columns) + 1) * (2 * (rem % 2) - 1), 0)
        flip = jnp.where(late, rem // 2, k)
        return dz, flip

    def needs(self, source, target):
        return jnp.abs(source - target) <= self.reach


def block_moves(place, kvbuf, send_sem, recv_sem, dz, flip, half, rows):
    z, y, core = place.z, place.y, place.core
    source_z = z + dz
    source = place.index(source_z, (y + flip) % 2 if place.columns == 2 else y, core)
    held = (source_z >= 0) & (source_z < place.planes) & place.needs(source, place.me)
    piece = kvbuf.at[source, pl.ds(half * rows, rows)]
    slot = (dz + place.far) * place.columns + flip
    edge = (source_z == 0) | (source_z == place.planes - 1)
    away = jnp.abs(dz)

    def along_z(distance):
        return (distance == 1) & (edge | (half == 1))

    def copy(kind, target):
        return pltpu.make_async_remote_copy(
            src_ref=piece,
            dst_ref=piece,
            send_sem=send_sem.at[kind, slot, half],
            recv_sem=recv_sem.at[source, half],
            device_id={"seq": target},
            device_id_type=MESH,
        )

    moves = []
    for kind, turn in ((0, 1), (1, -1)):
        target = jnp.clip(place.index(z + turn, y, core), 0, place.count - 1)
        go = held & (z + turn >= 0) & (z + turn < place.planes)
        go = go & (dz * turn <= 0) & (away + 1 <= place.far) & place.needs(source, target)
        go = go & ((flip == 0) | along_z(away + 1))
        moves.append((go, copy(kind, target)))
    if place.columns == 2:
        target = place.index(z, 1 - y, core)
        go = held & (flip == 0) & ((dz == 0) | jnp.logical_not(along_z(away)))
        moves.append((go & place.needs(source, target), copy(2, target)))
    target = place.index(z, y, 1 - core)
    moves.append((held & place.needs(source, target), copy(3, target)))
    return source, held, moves


def gelu(v):
    return 0.5 * v * (1.0 + lax.erf(v * math.sqrt(0.5)))


def layer_kernel(
    columns,
    count,
    act_hbm,
    taps_hbm,
    mix_hbm,
    wq_hbm,
    wkv_hbm,
    tiles_ref,
    codes_ref,
    valid_ref,
    out_ref,
    act,
    taps,
    mix,
    wq,
    wkv,
    halo,
    lifted,
    squeezed,
    mixed,
    normed,
    table,
    queries,
    scores_buf,
    probs_buf,
    kvbuf,
    peak,
    total,
    weighted,
    load_sem,
    halo_send,
    halo_recv,
    send_sem,
    recv_sem,
):
    rows, channels = act.shape
    hidden = mix.shape[0]
    half_rows = rows // 2
    tile = table.shape[1]
    tiles = rows // tile
    offsets = codes_ref.shape[1]
    edge = halo.shape[1]
    place = Place(count, columns, HALF // rows)
    me, z, y, core = place.me, place.z, place.y, place.core

    loads = [
        pltpu.make_async_copy(act_hbm, act, load_sem.at[0]),
        pltpu.make_async_copy(taps_hbm.at[0], taps.at[0], load_sem.at[1]),
        pltpu.make_async_copy(taps_hbm.at[1], taps.at[1], load_sem.at[2]),
        pltpu.make_async_copy(taps_hbm.at[2], taps.at[2], load_sem.at[3]),
        pltpu.make_async_copy(mix_hbm, mix, load_sem.at[4]),
        pltpu.make_async_copy(wq_hbm, wq, load_sem.at[5]),
        pltpu.make_async_copy(wkv_hbm, wkv, load_sem.at[6]),
    ]
    for load in loads:
        load.start()

    barrier = pltpu.get_barrier_semaphore()
    greeted = [(jnp.bool_(True), place.index(z, y, 1 - core))]
    if columns == 2:
        greeted.append((jnp.bool_(True), place.index(z, 1 - y, core)))
    for turn in (1, -1):
        ok = (z + turn >= 0) & (z + turn < place.planes)
        greeted.append((ok, jnp.clip(place.index(z + turn, y, core), 0, count - 1)))
    beyond = me + 2 * core - 1
    greeted.append(((beyond >= 0) & (beyond < count), jnp.clip(beyond, 0, count - 1)))
    for ok, target in greeted:

        @pl.when(ok)
        def _():
            pl.semaphore_signal(barrier, inc=1, device_id={"seq": target}, device_id_type=MESH)

    loads[0].wait()
    pl.semaphore_wait(barrier, sum(ok.astype(jnp.int32) for ok, _target in greeted))

    has_next = me + 1 < count
    has_prev = me > 0
    to_next = pltpu.make_async_remote_copy(
        src_ref=act.at[pl.ds(rows - edge, edge)],
        dst_ref=halo.at[0],
        send_sem=halo_send.at[0],
        recv_sem=halo_recv.at[0],
        device_id={"seq": jnp.minimum(me + 1, count - 1)},
        device_id_type=MESH,
    )
    to_prev = pltpu.make_async_remote_copy(
        src_ref=act.at[pl.ds(0, edge)],
        dst_ref=halo.at[1],
        send_sem=halo_send.at[1],
        recv_sem=halo_recv.at[1],
        device_id={"seq": jnp.maximum(me - 1, 0)},
        device_id_type=MESH,
    )

    @pl.when(has_next)
    def _():
        to_next.start()

    @pl.when(has_prev)
    def _():
        to_prev.start()

    table[...] = tiles_ref[...].astype(jnp.float32) * LOG2E
    peak[...] = jnp.full(peak.shape, masked_score, jnp.float32)
    total[...] = jnp.zeros(total.shape, jnp.float32)
    weighted[...] = jnp.zeros(weighted.shape, jnp.float32)

    def lift(strip, carry):
        at = pl.multiple_of(strip * edge, edge)
        lifted[pl.ds(at + edge, edge)] = gelu(act[pl.ds(at, edge)].astype(jnp.float32)).astype(
            jnp.bfloat16
        )
        return carry

    lax.fori_loop(0, rows // edge, lift, 0)

    for side, there, copy in ((0, has_prev, to_next), (1, has_next, to_prev)):
        at = side * (rows + edge)

        @pl.when(there)
        def _():
            copy.wait_recv()
            lifted[at : at + edge] = gelu(halo[side].astype(jnp.float32)).astype(jnp.bfloat16)

        @pl.when(jnp.logical_not(there))
        def _():
            lifted[at : at + edge] = jnp.zeros((edge, channels), jnp.bfloat16)

    def moves_of(k, half):
        dz, flip = place.step(k)
        return block_moves(place, kvbuf, send_sem, recv_sem, dz, flip, half, half_rows)

    def hand_on(held, moves):
        for go, copy in moves:

            @pl.when(go & held)
            def _():
                copy.start()

    for load in loads[1:]:
        load.wait()

    wide = 256
    shift = CONV_DILATION

    def front(half, carry):
        at = pl.multiple_of(half * half_rows, half_rows)
        tall = half_rows + edge
        for n in range(0, hidden, wide):
            low = jnp.dot(
                lifted[pl.ds(at, tall)],
                taps[0, :, n : n + wide],
                preferred_element_type=jnp.float32,
            )
            mid = jnp.dot(
                lifted[pl.ds(at + edge, half_rows)],
                taps[1, :, n : n + wide],
                preferred_element_type=jnp.float32,
            )
            high = jnp.dot(
                lifted[pl.ds(at + edge, tall)],
                taps[2, :, n : n + wide],
                preferred_element_type=jnp.float32,
            )
            conv = low[edge - shift : edge - shift + half_rows] + mid
            conv = conv + high[shift : shift + half_rows]
            squeezed[:, n : n + wide] = gelu(conv).astype(jnp.bfloat16)
        square = jnp.zeros((half_rows, 128), jnp.float32)
        for n in range(0, channels, wide):
            part = act[pl.ds(at, half_rows), n : n + wide].astype(jnp.float32) + jnp.dot(
                squeezed[...], mix[:, n : n + wide], preferred_element_type=jnp.float32
            )
            mixed[:, n : n + wide] = part
            for m in range(0, wide, 128):
                square = square + part[:, m : m + 128] * part[:, m : m + 128]
        mean = jnp.sum(square, axis=1, keepdims=True) * (1.0 / channels)
        factor = lax.rsqrt(mean + norm_eps)
        for n in range(0, channels, wide):
            normed[:, n : n + wide] = (mixed[:, n : n + wide] * factor).astype(jnp.bfloat16)
        keyval = jnp.dot(normed[...], wkv[...], preferred_element_type=jnp.float32)
        kvbuf[me, pl.ds(at, half_rows)] = keyval.astype(jnp.bfloat16)
        _source, held, moves = moves_of(0, half)
        hand_on(held, moves)
        query = jnp.dot(normed[...], wq[...], preferred_element_type=jnp.float32)
        queries[pl.ds(at, half_rows)] = (query * (LOG2E / math.sqrt(HDIM))).astype(jnp.bfloat16)
        return carry

    lax.fori_loop(0, 2, front, 0)

    strip_rows = 32

    def absorb(source, special):
        delta = source - me
        scores_buf[...] = lax.dot_general(
            queries[...],
            kvbuf[source, :, :HDIM],
            (((1,), (1,)), ((), ())),
            preferred_element_type=jnp.float32,
        )
        shrinks = []
        for i in range(tiles):
            codes = []
            for j in range(tiles):
                offset = jnp.clip(delta * tiles + (j - i) + offsets // 2, 0, offsets - 1)
                codes.append(codes_ref[i, offset])
            for r in range(0, tile, strip_rows):
                at = i * tile + r
                bias = jnp.concatenate(
                    [table[code, r : r + strip_rows] for code in codes], axis=1
                )
                scores = scores_buf[at : at + strip_rows] + bias
                if special:
                    row = lax.broadcasted_iota(jnp.int32, (strip_rows, rows), 0) + at
                    col = lax.broadcasted_iota(jnp.int32, (strip_rows, rows), 1)
                    apart = delta * rows + col - row
                    kept = (jnp.abs(apart) <= HALF) & (valid_ref[source] >= 0.0)
                    scores = jnp.where((apart == 0) | kept, scores, masked_score)
                else:
                    scores = scores + valid_ref[source]
                old = peak[at : at + strip_rows]
                new = jnp.maximum(old, jnp.max(scores, axis=1, keepdims=True))
                probs = jnp.exp2(scores - new)
                shrink = jnp.exp2(old - new)
                peak[at : at + strip_rows] = new
                total[at : at + strip_rows] = total[at : at + strip_rows] * shrink + jnp.sum(
                    probs, axis=1, keepdims=True
                )
                weighted[at : at + strip_rows] = weighted[at : at + strip_rows] * shrink
                probs_buf[at : at + strip_rows] = probs.astype(jnp.bfloat16)
        weighted[...] += jnp.dot(
            probs_buf[...], kvbuf[source, :, HDIM:], preferred_element_type=jnp.float32
        )

    def absorb_block(source):
        apart = jnp.abs(source - me)
        special = (apart == 0) | (apart == place.reach)

        @pl.when(special)
        def _():
            absorb(source, True)

        @pl.when(jnp.logical_not(special))
        def _():
            absorb(source, False)

    def arrived(source, half):
        piece = kvbuf.at[source, pl.ds(half * half_rows, half_rows)]
        pltpu.make_async_copy(piece, piece, recv_sem.at[source, half]).wait()

    def turn_of(k, carry):
        for half in range(2):
            source, held, moves = moves_of(k, half)
            held = held & (k < place.steps)

            @pl.when(held & (k > 0))
            def _():
                arrived(source, half)

            hand_on(held & (k > 0), moves)

        dz, flip = place.step(jnp.maximum(k - 1, 0))
        other_z = z + dz
        other = place.index(other_z, (y + flip) % 2 if columns == 2 else y, 1 - core)
        take = (k > 0) & (other_z >= 0) & (other_z < place.planes) & place.needs(other, me)

        @pl.when(held)
        def _():
            absorb_block(source)

        @pl.when(take)
        def _():
            arrived(other, 0)
            arrived(other, 1)
            absorb_block(other)

        return carry

    lax.fori_loop(0, place.steps + 1, turn_of, 0)
    out_ref[...] = (weighted[...] / total[...]).astype(out_ref.dtype)

    def drain(k, carry):
        for half in range(2):
            _source, _held, moves = moves_of(k, half)
            for go, copy in moves:

                @pl.when(go)
                def _():
                    copy.wait_send()

        return carry

    lax.fori_loop(0, place.steps, drain, 0)

    @pl.when(has_next)
    def _():
        to_next.wait_send()

    @pl.when(has_prev)
    def _():
        to_prev.wait_send()


def per_device(
    columns,
    activations,
    dilated_tap_weight,
    conv_mix,
    w_query,
    w_keyval,
    contact_tiles,
    tile_codes,
    bin_valid,
):
    rows, channels = activations.shape
    hidden = conv_mix.shape[0]
    half_rows = rows // 2
    edge = 16
    count = lax.axis_size("seq")
    plane = 2 * columns
    far = -(-(HALF // rows) // plane)
    valid = jnp.where(bin_valid == 1, 0.0, masked_score).astype(jnp.float32)
    valid = valid.reshape(count, 1, rows)
    vmem = pl.BlockSpec(memory_space=pltpu.VMEM)
    smem = pl.BlockSpec(memory_space=pltpu.SMEM)
    hbm = pl.BlockSpec(memory_space=pl.ANY)
    bf16, f32 = jnp.bfloat16, jnp.float32
    return pl.pallas_call(
        functools.partial(layer_kernel, columns, count),
        out_shape=jax.ShapeDtypeStruct((rows, HDIM), bf16),
        in_specs=[hbm, hbm, hbm, hbm, hbm, vmem, smem, vmem],
        out_specs=vmem,
        scratch_shapes=[
            pltpu.VMEM(activations.shape, bf16),
            pltpu.VMEM(dilated_tap_weight.shape, bf16),
            pltpu.VMEM(conv_mix.shape, bf16),
            pltpu.VMEM(w_query.shape, bf16),
            pltpu.VMEM(w_keyval.shape, bf16),
            pltpu.VMEM((2, edge, channels), bf16),
            pltpu.VMEM((rows + 2 * edge, channels), bf16),
            pltpu.VMEM((half_rows, hidden), bf16),
            pltpu.VMEM((half_rows, channels), f32),
            pltpu.VMEM((half_rows, channels), bf16),
            pltpu.VMEM(contact_tiles.shape, f32),
            pltpu.VMEM((rows, HDIM), bf16),
            pltpu.VMEM((rows, rows), f32),
            pltpu.VMEM((rows, rows), bf16),
            pltpu.VMEM((count, rows, 2 * HDIM), bf16),
            pltpu.VMEM((rows, 1), f32),
            pltpu.VMEM((rows, 1), f32),
            pltpu.VMEM((rows, HDIM), f32),
            pltpu.SemaphoreType.DMA((7,)),
            pltpu.SemaphoreType.DMA((2,)),
            pltpu.SemaphoreType.DMA((2,)),
            pltpu.SemaphoreType.DMA((4, (2 * far + 1) * columns, 2)),
            pltpu.SemaphoreType.DMA((count, 2)),
        ],
        compiler_params=pltpu.CompilerParams(
            collective_id=0, has_side_effects=True, vmem_limit_bytes=56 * 1024 * 1024
        ),
        cost_estimate=pl.CostEstimate(
            flops=2 * rows * channels * (4 * hidden + 3 * HDIM) + 4 * rows * HDIM * 2 * HALF,
            bytes_accessed=14 * 1024 * 1024,
            transcendentals=rows * 2 * HALF,
        ),
    )(
        activations,
        dilated_tap_weight,
        conv_mix,
        w_query,
        w_keyval,
        contact_tiles,
        tile_codes,
        valid,
    )


def columns_of(mesh):
    along = mesh.devices.reshape(-1, mesh.shape["seq"])[0]
    first = along[0]
    if not hasattr(first, "coords"):
        return 2 if mesh.shape["seq"] == 16 else 1
    return sum(d.coords[2] == first.coords[2] for d in along) // 2


def solution(mesh):
    in_specs = (P(("grp", "seq"), None), P(), P(), P(), P(), P(), P(("grp", "seq"), None), P("grp"))
    out_specs = P(("grp", "seq"), None)
    return jax.shard_map(
        functools.partial(per_device, columns_of(mesh)),
        mesh=mesh,
        in_specs=in_specs,
        out_specs=out_specs,
        check_vma=False,
    )
```

```python
import functools
import math

import jax
import jax.numpy as jnp
from jax import lax
from jax.experimental import pallas as pl
from jax.experimental.pallas import tpu as pltpu
from jax.sharding import PartitionSpec as P

HDIM = 128
CONV_DILATION = 8
HALF = 4096
MESH = pl.DeviceIdType.MESH

masked_score = -1e30
norm_eps = 1e-06
LOG2E = math.log2(math.e)


class Place:
    def __init__(self, count, columns, reach):
        self.count = count
        self.columns = columns
        self.plane = 2 * columns
        self.planes = count // self.plane
        self.reach = reach
        self.far = -(-reach // self.plane)
        self.steps = (2 * self.far + 1) * columns
        me = lax.axis_index("seq")
        self.me = me
        self.z = me // self.plane
        self.y = (me % self.plane) // 2
        self.core = me % 2

    def index(self, z, y, core):
        return z * self.plane + y * 2 + core

    def order(self):
        blocks = [(0, 0)]
        late = [(0, 1)]
        for d in range(1, self.far + 1):
            if d == 1 and self.columns == 2:
                blocks += late
                late = []
            blocks += [(-d, 0), (d, 0)]
            if d > 1 and self.columns == 2:
                blocks += late
            late = [(-d, 1), (d, 1)]
        if self.columns == 2:
            blocks += late
        return blocks

    def hand_order(self):
        blocks = self.order()
        first = 3 if self.columns == 2 else 2
        steps = [(1, k, 0) for k in range(1, first + 1)]
        steps += [(2, k, 1) for k in range(1, first + 1)]
        k, turn = first + 1, 4
        while k < len(blocks):
            steps += [(turn, k, 0), (turn, k + 1, 0)]
            turn += 2
            steps += [(turn, k, 1), (turn, k + 1, 1)]
            k += 2
        assert all(turn <= 2 * k for turn, k, _half in steps)
        return steps

    def step(self, k):
        dz = flip = jnp.int32(0)
        for i, (d, f) in enumerate(self.order()):
            dz = jnp.where(k == i, d, dz)
            flip = jnp.where(k == i, f, flip)
        return dz, flip

    def needs(self, source, target):
        return jnp.abs(source - target) <= self.reach


def block_moves(place, kvbuf, send_sem, recv_sem, dz, flip, half, part):
    z, y, core = place.z, place.y, place.core
    source_z = z + dz
    source = place.index(source_z, (y + flip) % 2 if place.columns == 2 else y, core)
    held = (source_z >= 0) & (source_z < place.planes) & place.needs(source, place.me)
    piece = kvbuf.at[source, pl.ds(half * part, part)]
    slot = (dz + place.far) * place.columns + flip
    edge = (source_z == 0) | (source_z == place.planes - 1)
    away = jnp.abs(dz)

    def along_z(distance):
        return (distance == 1) & (edge | (half == 1))

    def copy(kind, target):
        return pltpu.make_async_remote_copy(
            src_ref=piece,
            dst_ref=piece,
            send_sem=send_sem.at[kind, slot, half],
            recv_sem=recv_sem.at[source, half],
            device_id={"seq": target},
            device_id_type=MESH,
        )

    moves = []
    for kind, turn in ((0, 1), (1, -1)):
        target = jnp.clip(place.index(z + turn, y, core), 0, place.count - 1)
        go = held & (z + turn >= 0) & (z + turn < place.planes)
        go = go & (dz * turn <= 0) & (away + 1 <= place.far) & place.needs(source, target)
        go = go & ((flip == 0) | along_z(away + 1))
        moves.append((go, copy(kind, target)))
    if place.columns == 2:
        target = place.index(z, 1 - y, core)
        go = held & (flip == 0) & ((dz == 0) | jnp.logical_not(along_z(away)))
        moves.append((go & place.needs(source, target), copy(2, target)))
    target = place.index(z, y, 1 - core)
    moves.append((held & place.needs(source, target), copy(3, target)))
    return source, held, moves


def gelu(v):
    size = jnp.abs(v)
    low = 1.0 + (0.3275911 * math.sqrt(0.5)) * size
    t = pl.reciprocal(low, approx=True)
    t = t * (2.0 - low * t)
    poly = 0.5 * 1.061405429 * t - 0.5 * 1.453152027
    poly = poly * t + 0.5 * 1.421413741
    poly = poly * t - 0.5 * 0.284496736
    poly = (poly * t + 0.5 * 0.254829592) * t
    tail = poly * jnp.exp2((-0.5 * LOG2E) * (size * size))
    return jnp.maximum(v, 0.0) - size * tail


def layer_kernel(
    columns,
    count,
    act_hbm,
    taps_hbm,
    mix_hbm,
    wq_hbm,
    wkv_hbm,
    mask_hbm,
    tiles_ref,
    codes_ref,
    out_ref,
    act,
    taps,
    mix,
    wq,
    wkv,
    halo,
    lifted,
    squeezed,
    mixed,
    normed,
    table,
    queries,
    mask,
    scores_buf,
    probs_buf,
    kvbuf,
    peak,
    weighted,
    load_sem,
    halo_send,
    halo_recv,
    send_sem,
    recv_sem,
):
    rows, channels = act.shape
    hidden = mix.shape[0]
    half_rows = rows // 2
    tile = table.shape[1]
    tiles = rows // tile
    offsets = codes_ref.shape[1]
    edge = halo.shape[1]
    place = Place(count, columns, HALF // rows)
    me, z, y, core = place.me, place.z, place.y, place.core

    loads = [
        pltpu.make_async_copy(act_hbm, act, load_sem.at[0]),
        pltpu.make_async_copy(taps_hbm.at[0], taps.at[0], load_sem.at[1]),
        pltpu.make_async_copy(taps_hbm.at[1], taps.at[1], load_sem.at[2]),
        pltpu.make_async_copy(taps_hbm.at[2], taps.at[2], load_sem.at[3]),
        pltpu.make_async_copy(mix_hbm, mix, load_sem.at[4]),
        pltpu.make_async_copy(wq_hbm, wq, load_sem.at[5]),
        pltpu.make_async_copy(wkv_hbm, wkv, load_sem.at[6]),
        pltpu.make_async_copy(mask_hbm, mask, load_sem.at[7]),
    ]
    for load in loads:
        load.start()

    barrier = pltpu.get_barrier_semaphore()
    greeted = [(jnp.bool_(True), place.index(z, y, 1 - core))]
    if columns == 2:
        greeted.append((jnp.bool_(True), place.index(z, 1 - y, core)))
    for turn in (1, -1):
        ok = (z + turn >= 0) & (z + turn < place.planes)
        greeted.append((ok, jnp.clip(place.index(z + turn, y, core), 0, count - 1)))
    beyond = me + 2 * core - 1
    greeted.append(((beyond >= 0) & (beyond < count), jnp.clip(beyond, 0, count - 1)))
    for ok, target in greeted:

        @pl.when(ok)
        def _():
            pl.semaphore_signal(barrier, inc=1, device_id={"seq": target}, device_id_type=MESH)

    loads[0].wait()
    pl.semaphore_wait(barrier, sum(ok.astype(jnp.int32) for ok, _target in greeted))

    has_next = me + 1 < count
    has_prev = me > 0
    to_next = pltpu.make_async_remote_copy(
        src_ref=act.at[pl.ds(rows - edge, edge)],
        dst_ref=halo.at[0],
        send_sem=halo_send.at[0],
        recv_sem=halo_recv.at[0],
        device_id={"seq": jnp.minimum(me + 1, count - 1)},
        device_id_type=MESH,
    )
    to_prev = pltpu.make_async_remote_copy(
        src_ref=act.at[pl.ds(0, edge)],
        dst_ref=halo.at[1],
        send_sem=halo_send.at[1],
        recv_sem=halo_recv.at[1],
        device_id={"seq": jnp.maximum(me - 1, 0)},
        device_id_type=MESH,
    )

    @pl.when(has_next)
    def _():
        to_next.start()

    @pl.when(has_prev)
    def _():
        to_prev.start()

    for code in range(tiles_ref.shape[0]):
        table[code] = tiles_ref[code].astype(jnp.float32).T * LOG2E
    peak[...] = jnp.full(peak.shape, masked_score, jnp.float32)
    spare = lax.broadcasted_iota(jnp.int32, (HDIM, rows), 0) == 0
    queries[HDIM:] = jnp.where(spare, 1.0, 0.0).astype(jnp.bfloat16)
    weighted[...] = jnp.zeros(weighted.shape, jnp.float32)

    def lift(strip, carry):
        at = pl.multiple_of(strip * 2 * edge, 2 * edge)
        raised = gelu(act[pl.ds(at, 2 * edge)].astype(jnp.float32))
        lifted[pl.ds(at + edge, 2 * edge)] = raised.astype(jnp.bfloat16)
        return carry

    lax.fori_loop(0, rows // (2 * edge), lift, 0)

    for side, there, copy in ((0, has_prev, to_next), (1, has_next, to_prev)):
        at = side * (rows + edge)

        @pl.when(there)
        def _():
            copy.wait_recv()
            lifted[at : at + edge] = gelu(halo[side].astype(jnp.float32)).astype(jnp.bfloat16)

        @pl.when(jnp.logical_not(there))
        def _():
            lifted[at : at + edge] = jnp.zeros((edge, channels), jnp.bfloat16)

    def moves_of(k, half):
        dz, flip = place.step(k)
        return block_moves(place, kvbuf, send_sem, recv_sem, dz, flip, half, tiles // 2)

    def hand_on(held, moves):
        for go, copy in moves:

            @pl.when(go & held)
            def _():
                copy.start()

    for load in loads[1:]:
        load.wait()

    wide = 256
    shift = CONV_DILATION

    def front(half, carry):
        at = pl.multiple_of(half * half_rows, half_rows)
        tall = half_rows + edge
        for n in range(0, hidden, wide):
            low = jnp.dot(
                lifted[pl.ds(at, tall)],
                taps[0, :, n : n + wide],
                preferred_element_type=jnp.float32,
            )
            mid = jnp.dot(
                lifted[pl.ds(at + edge, half_rows)],
                taps[1, :, n : n + wide],
                preferred_element_type=jnp.float32,
            )
            high = jnp.dot(
                lifted[pl.ds(at + edge, tall)],
                taps[2, :, n : n + wide],
                preferred_element_type=jnp.float32,
            )
            conv = low[edge - shift : edge - shift + half_rows] + mid
            conv = conv + high[shift : shift + half_rows]
            squeezed[:, n : n + wide] = gelu(conv).astype(jnp.bfloat16)
        square = jnp.zeros((half_rows, 128), jnp.float32)
        for n in range(0, channels, wide):
            part = act[pl.ds(at, half_rows), n : n + wide].astype(jnp.float32) + jnp.dot(
                squeezed[...], mix[:, n : n + wide], preferred_element_type=jnp.float32
            )
            mixed[:, n : n + wide] = part
            for m in range(0, wide, 128):
                square = square + part[:, m : m + 128] * part[:, m : m + 128]
        mean = jnp.sum(square, axis=1, keepdims=True) * (1.0 / channels)
        factor = lax.rsqrt(mean + norm_eps)
        for n in range(0, channels, wide):
            normed[:, n : n + wide] = (mixed[:, n : n + wide] * factor).astype(jnp.bfloat16)
        keyval = jnp.dot(normed[...], wkv[...], preferred_element_type=jnp.float32)
        keys = keyval[:, :HDIM].astype(jnp.bfloat16)
        values = keyval[:, HDIM:].T.astype(jnp.bfloat16)
        for j in range(tiles // 2):
            here = slice(j * tile, (j + 1) * tile)
            kvbuf[me, half * (tiles // 2) + j, :tile] = keys[here]
            kvbuf[me, half * (tiles // 2) + j, tile:] = values[:, here]
        _source, held, moves = moves_of(0, half)
        hand_on(held, moves)
        query = jnp.dot(normed[...], wq[...], preferred_element_type=jnp.float32)
        query = (query * (LOG2E / math.sqrt(HDIM))).T.astype(jnp.bfloat16)

        @pl.when(half == 0)
        def _():
            queries[:HDIM, :half_rows] = query

        @pl.when(half == 1)
        def _():
            queries[:HDIM, half_rows:] = query

        return carry

    lax.fori_loop(0, 2, front, 0)

    def absorb(source, special):
        delta = source - me
        keys = jnp.concatenate([kvbuf[source, j, :tile] for j in range(tiles)], axis=0)
        values = jnp.concatenate([kvbuf[source, j, tile:] for j in range(tiles)], axis=1)
        values = jnp.concatenate([values, jnp.ones((16, rows), jnp.bfloat16)], axis=0)
        if special:
            scores_buf[...] = jnp.dot(
                keys, queries[:HDIM], preferred_element_type=jnp.float32
            )
        else:
            keys = jnp.concatenate([keys, mask[source]], axis=1)
            scores_buf[...] = jnp.dot(keys, queries[...], preferred_element_type=jnp.float32)
        shrinks = []
        for i in range(tiles):
            across = slice(i * tile, (i + 1) * tile)
            column = []
            for j in range(tiles):
                offset = jnp.clip(delta * tiles + (j - i) + offsets // 2, 0, offsets - 1)
                scores = scores_buf[j * tile : (j + 1) * tile, across] + table[codes_ref[i, offset]]
                if special:
                    key_row = lax.broadcasted_iota(jnp.int32, (tile, tile), 0) + j * tile
                    query_row = lax.broadcasted_iota(jnp.int32, (tile, tile), 1) + i * tile
                    apart = delta * rows + key_row - query_row
                    usable = mask[source, j * tile : (j + 1) * tile].astype(jnp.float32) >= 0.0
                    kept = (apart == 0) | ((jnp.abs(apart) <= HALF) & usable)
                    scores = jnp.where(kept, scores, masked_score)
                column.append(scores)
            column = jnp.concatenate(column, axis=0)
            old = peak[:, across]
            new = jnp.maximum(old, jnp.max(column, axis=0, keepdims=True))
            probs_buf[:, across] = jnp.exp2(column - new).astype(jnp.bfloat16)
            peak[:, across] = new
            shrinks.append(jnp.exp2(old - new))
        shrink = jnp.concatenate(shrinks, axis=1)
        weighted[...] = weighted[...] * shrink + jnp.dot(
            values, probs_buf[...], preferred_element_type=jnp.float32
        )

    def absorb_block(source):
        apart = jnp.abs(source - me)
        special = (apart == 0) | (apart == place.reach)

        @pl.when(special)
        def _():
            absorb(source, True)

        @pl.when(jnp.logical_not(special))
        def _():
            absorb(source, False)

    def arrived(source, half):
        piece = kvbuf.at[source, pl.ds(half * (tiles // 2), tiles // 2)]
        pltpu.make_async_copy(piece, piece, recv_sem.at[source, half]).wait()

    hand_steps = place.hand_order()
    turns = 2 * place.steps

    def hand_one(c, carry):
        k = half = jnp.int32(0)
        for i, (_turn, block, part) in enumerate(hand_steps):
            k = jnp.where(c == i, block, k)
            half = jnp.where(c == i, part, half)
        source, held, moves = moves_of(k, half)

        @pl.when(held)
        def _():
            arrived(source, half)

        hand_on(held, moves)
        return carry

    def turn_of(u, done):
        until = jnp.int32(0)
        for turn, _block, _part in hand_steps:
            until = until + jnp.where(turn <= u, 1, 0)
        lax.fori_loop(done, until, hand_one, 0)
        dz, flip = place.step(u // 2)
        away = u % 2
        source_z = z + dz
        column = (y + flip) % 2 if columns == 2 else y
        source = place.index(source_z, column, (core + away) % 2)
        take = (source_z >= 0) & (source_z < place.planes) & place.needs(source, me)

        @pl.when(take)
        def _():
            @pl.when(away == 1)
            def _():
                arrived(source, 0)
                arrived(source, 1)

            absorb_block(source)

        return until

    lax.fori_loop(0, turns, turn_of, jnp.int32(0))
    result = weighted[:HDIM] / weighted[HDIM : HDIM + 1]
    out_ref[...] = result.T.astype(out_ref.dtype)

    def drain(k, carry):
        for half in range(2):
            _source, _held, moves = moves_of(k, half)
            for go, copy in moves:

                @pl.when(go)
                def _():
                    copy.wait_send()

        return carry

    lax.fori_loop(0, place.steps, drain, 0)

    @pl.when(has_next)
    def _():
        to_next.wait_send()

    @pl.when(has_prev)
    def _():
        to_prev.wait_send()


def per_device(
    columns,
    activations,
    dilated_tap_weight,
    conv_mix,
    w_query,
    w_keyval,
    contact_tiles,
    tile_codes,
    bin_valid,
):
    rows, channels = activations.shape
    hidden = conv_mix.shape[0]
    half_rows = rows // 2
    edge = 16
    tile = contact_tiles.shape[1]
    count = lax.axis_size("seq")
    plane = 2 * columns
    far = -(-(HALF // rows) // plane)
    mask = jnp.where(bin_valid == 1, 0.0, masked_score).astype(jnp.bfloat16)
    mask = jnp.broadcast_to(mask.reshape(count, rows, 1), (count, rows, HDIM))
    vmem = pl.BlockSpec(memory_space=pltpu.VMEM)
    smem = pl.BlockSpec(memory_space=pltpu.SMEM)
    hbm = pl.BlockSpec(memory_space=pl.ANY)
    bf16, f32 = jnp.bfloat16, jnp.float32
    return pl.pallas_call(
        functools.partial(layer_kernel, columns, count),
        out_shape=jax.ShapeDtypeStruct((rows, HDIM), bf16),
        in_specs=[hbm, hbm, hbm, hbm, hbm, hbm, vmem, smem],
        out_specs=vmem,
        scratch_shapes=[
            pltpu.VMEM(activations.shape, bf16),
            pltpu.VMEM(dilated_tap_weight.shape, bf16),
            pltpu.VMEM(conv_mix.shape, bf16),
            pltpu.VMEM(w_query.shape, bf16),
            pltpu.VMEM(w_keyval.shape, bf16),
            pltpu.VMEM((2, edge, channels), bf16),
            pltpu.VMEM((rows + 2 * edge, channels), bf16),
            pltpu.VMEM((half_rows, hidden), bf16),
            pltpu.VMEM((half_rows, channels), f32),
            pltpu.VMEM((half_rows, channels), bf16),
            pltpu.VMEM(contact_tiles.shape, f32),
            pltpu.VMEM((2 * HDIM, rows), bf16),
            pltpu.VMEM(mask.shape, bf16),
            pltpu.VMEM((rows, rows), f32),
            pltpu.VMEM((rows, rows), bf16),
            pltpu.VMEM((count, rows // tile, 2 * tile, HDIM), bf16),
            pltpu.VMEM((1, rows), f32),
            pltpu.VMEM((HDIM + 16, rows), f32),
            pltpu.SemaphoreType.DMA((8,)),
            pltpu.SemaphoreType.DMA((2,)),
            pltpu.SemaphoreType.DMA((2,)),
            pltpu.SemaphoreType.DMA((4, (2 * far + 1) * columns, 2)),
            pltpu.SemaphoreType.DMA((count, 2)),
        ],
        compiler_params=pltpu.CompilerParams(
            collective_id=0, has_side_effects=True, vmem_limit_bytes=56 * 1024 * 1024
        ),
        cost_estimate=pl.CostEstimate(
            flops=2 * rows * channels * (4 * hidden + 3 * HDIM) + 4 * rows * HDIM * 2 * HALF,
            bytes_accessed=14 * 1024 * 1024,
            transcendentals=rows * 2 * HALF,
        ),
    )(
        activations,
        dilated_tap_weight,
        conv_mix,
        w_query,
        w_keyval,
        mask,
        contact_tiles,
        tile_codes,
    )


def columns_of(mesh):
    along = mesh.devices.reshape(-1, mesh.shape["seq"])[0]
    first = along[0]
    if not hasattr(first, "coords"):
        return 2 if mesh.shape["seq"] == 16 else 1
    return sum(d.coords[2] == first.coords[2] for d in along) // 2


def solution(mesh):
    in_specs = (P(("grp", "seq"), None), P(), P(), P(), P(), P(), P(("grp", "seq"), None), P("grp"))
    out_specs = P(("grp", "seq"), None)
    return jax.shard_map(
        functools.partial(per_device, columns_of(mesh)),
        mesh=mesh,
        in_specs=in_specs,
        out_specs=out_specs,
        check_vma=False,
    )
```

```python
import functools
import math

import jax
import jax.numpy as jnp
from jax import lax
from jax.experimental import pallas as pl
from jax.experimental.pallas import tpu as pltpu
from jax.sharding import PartitionSpec as P

HDIM = 128
CONV_DILATION = 8
HALF = 4096
MESH = pl.DeviceIdType.MESH

masked_score = -1e30
norm_eps = 1e-06
LOG2E = math.log2(math.e)


class Place:
    def __init__(self, count, columns, reach):
        self.count = count
        self.columns = columns
        self.plane = 2 * columns
        self.planes = count // self.plane
        self.reach = reach
        self.far = -(-reach // self.plane)
        self.steps = (2 * self.far + 1) * columns
        me = lax.axis_index("seq")
        self.me = me
        self.z = me // self.plane
        self.y = (me % self.plane) // 2
        self.core = me % 2

    def index(self, z, y, core):
        return z * self.plane + y * 2 + core

    def order(self):
        blocks = [(0, 0)]
        late = [(0, 1)]
        for d in range(1, self.far + 1):
            if d == 1 and self.columns == 2:
                blocks += late
                late = []
            blocks += [(-d, 0), (d, 0)]
            if d > 1 and self.columns == 2:
                blocks += late
            late = [(-d, 1), (d, 1)]
        if self.columns == 2:
            blocks += late
        return blocks

    def hand_order(self):
        blocks = self.order()
        first = self.near()
        steps = [(0, k, 0) for k in range(1, first + 1)]
        steps += [(2, k, 1) for k in range(1, first + 1)]
        for k in range(first + 1, len(blocks), 2):
            early = 2 if self.columns == 2 and k == first + 1 else 0
            steps += [(2 * k - 2 - early, k, 0), (2 * k - 2 - early, k + 1, 0)]
            steps += [(2 * k - early, k, 1), (2 * k - early, k + 1, 1)]
        return steps

    def near(self):
        return 3 if self.columns == 2 else 2

    def step(self, k):
        dz = flip = jnp.int32(0)
        for i, (d, f) in enumerate(self.order()):
            dz = jnp.where(k == i, d, dz)
            flip = jnp.where(k == i, f, flip)
        return dz, flip

    def needs(self, source, target):
        return jnp.abs(source - target) <= self.reach


def block_moves(place, kvbuf, send_sem, recv_sem, dz, flip, half, part):
    z, y, core = place.z, place.y, place.core
    source_z = z + dz
    source = place.index(source_z, (y + flip) % 2 if place.columns == 2 else y, core)
    held = (source_z >= 0) & (source_z < place.planes) & place.needs(source, place.me)
    piece = kvbuf.at[source, pl.ds(half * part, part)]
    slot = (dz + place.far) * place.columns + flip
    edge = (source_z == 0) | (source_z == place.planes - 1)
    away = jnp.abs(dz)

    def along_z(distance):
        return (distance == 1) & (edge | (half == 1))

    def copy(kind, target):
        return pltpu.make_async_remote_copy(
            src_ref=piece,
            dst_ref=piece,
            send_sem=send_sem.at[kind, slot, half],
            recv_sem=recv_sem.at[source, half],
            device_id={"seq": target},
            device_id_type=MESH,
        )

    moves = []
    for kind, turn in ((0, 1), (1, -1)):
        target = jnp.clip(place.index(z + turn, y, core), 0, place.count - 1)
        go = held & (z + turn >= 0) & (z + turn < place.planes)
        go = go & (dz * turn <= 0) & (away + 1 <= place.far) & place.needs(source, target)
        go = go & ((flip == 0) | along_z(away + 1))
        moves.append((go, copy(kind, target)))
    if place.columns == 2:
        target = place.index(z, 1 - y, core)
        go = held & (flip == 0) & ((dz == 0) | jnp.logical_not(along_z(away)))
        moves.append((go & place.needs(source, target), copy(2, target)))
    target = place.index(z, y, 1 - core)
    moves.append((held & place.needs(source, target), copy(3, target)))
    return source, held, moves


def gelu(v):
    size = jnp.abs(v)
    low = 1.0 + (0.3275911 * math.sqrt(0.5)) * size
    t = pl.reciprocal(low, approx=True)
    t = t * (2.0 - low * t)
    poly = 0.5 * 1.061405429 * t - 0.5 * 1.453152027
    poly = poly * t + 0.5 * 1.421413741
    poly = poly * t - 0.5 * 0.284496736
    poly = (poly * t + 0.5 * 0.254829592) * t
    tail = poly * jnp.exp2((-0.5 * LOG2E) * (size * size))
    return jnp.maximum(v, 0.0) - size * tail


def layer_kernel(
    columns,
    count,
    act_hbm,
    taps_hbm,
    mix_hbm,
    wq_hbm,
    wkv_hbm,
    tiles_ref,
    codes_ref,
    valid_ref,
    out_ref,
    act,
    taps,
    mix,
    wq,
    wkv,
    halo,
    lifted,
    squeezed,
    mixed,
    normed,
    table,
    queries,
    scores_buf,
    probs_buf,
    kvbuf,
    peak,
    weighted,
    load_sem,
    halo_send,
    halo_recv,
    send_sem,
    recv_sem,
):
    rows, channels = act.shape
    hidden = mix.shape[0]
    half_rows = rows // 2
    tile = table.shape[1]
    tiles = rows // tile
    offsets = codes_ref.shape[1]
    edge = halo.shape[1]
    early_rows = half_rows + 2 * edge
    place = Place(count, columns, HALF // rows)
    me, z, y, core = place.me, place.z, place.y, place.core

    loads = [
        pltpu.make_async_copy(
            act_hbm.at[pl.ds(0, early_rows)], act.at[pl.ds(0, early_rows)], load_sem.at[0]
        ),
        pltpu.make_async_copy(
            act_hbm.at[pl.ds(early_rows, rows - early_rows)],
            act.at[pl.ds(early_rows, rows - early_rows)],
            load_sem.at[7],
        ),
        pltpu.make_async_copy(taps_hbm.at[0], taps.at[0], load_sem.at[1]),
        pltpu.make_async_copy(taps_hbm.at[1], taps.at[1], load_sem.at[2]),
        pltpu.make_async_copy(taps_hbm.at[2], taps.at[2], load_sem.at[3]),
        pltpu.make_async_copy(mix_hbm, mix, load_sem.at[4]),
        pltpu.make_async_copy(wq_hbm, wq, load_sem.at[5]),
        pltpu.make_async_copy(wkv_hbm, wkv, load_sem.at[6]),
    ]
    for load in loads:
        load.start()

    barrier = pltpu.get_barrier_semaphore()
    greeted = [(jnp.bool_(True), place.index(z, y, 1 - core))]
    if columns == 2:
        greeted.append((jnp.bool_(True), place.index(z, 1 - y, core)))
    for turn in (1, -1):
        ok = (z + turn >= 0) & (z + turn < place.planes)
        greeted.append((ok, jnp.clip(place.index(z + turn, y, core), 0, count - 1)))
    beyond = me + 2 * core - 1
    greeted.append(((beyond >= 0) & (beyond < count), jnp.clip(beyond, 0, count - 1)))
    for ok, target in greeted:

        @pl.when(ok)
        def _():
            pl.semaphore_signal(barrier, inc=1, device_id={"seq": target}, device_id_type=MESH)

    loads[0].wait()
    loads[1].wait()
    pl.semaphore_wait(barrier, sum(ok.astype(jnp.int32) for ok, _target in greeted))

    has_next = me + 1 < count
    has_prev = me > 0
    to_next = pltpu.make_async_remote_copy(
        src_ref=act.at[pl.ds(rows - edge, edge)],
        dst_ref=halo.at[0],
        send_sem=halo_send.at[0],
        recv_sem=halo_recv.at[0],
        device_id={"seq": jnp.minimum(me + 1, count - 1)},
        device_id_type=MESH,
    )
    to_prev = pltpu.make_async_remote_copy(
        src_ref=act.at[pl.ds(0, edge)],
        dst_ref=halo.at[1],
        send_sem=halo_send.at[1],
        recv_sem=halo_recv.at[1],
        device_id={"seq": jnp.maximum(me - 1, 0)},
        device_id_type=MESH,
    )

    @pl.when(has_next)
    def _():
        to_next.start()

    @pl.when(has_prev)
    def _():
        to_prev.start()

    peak[...] = jnp.full(peak.shape, masked_score, jnp.float32)
    spare = lax.broadcasted_iota(jnp.int32, (HDIM, rows), 0) == 0
    queries[HDIM:] = jnp.where(spare, 1.0, 0.0).astype(jnp.bfloat16)
    weighted[...] = jnp.zeros(weighted.shape, jnp.float32)

    def lift(at, count):
        raised = gelu(act[pl.ds(at, count)].astype(jnp.float32))
        lifted[pl.ds(at + edge, count)] = raised.astype(jnp.bfloat16)

    def lift_strip(strip, carry):
        lift(pl.multiple_of(strip * 2 * edge, 2 * edge), 2 * edge)
        return carry

    def turn_tile(code):
        table[code] = tiles_ref[code].astype(jnp.float32).T * LOG2E

    lax.fori_loop(0, early_rows // (2 * edge), lift_strip, 0)

    def lift_halo(side, there, copy):
        at = side * (rows + edge)

        @pl.when(there)
        def _():
            copy.wait_recv()
            lifted[at : at + edge] = gelu(halo[side].astype(jnp.float32)).astype(jnp.bfloat16)

        @pl.when(jnp.logical_not(there))
        def _():
            lifted[at : at + edge] = jnp.zeros((edge, channels), jnp.bfloat16)

    lift_halo(0, has_prev, to_next)

    def moves_of(k, half):
        dz, flip = place.step(k)
        return block_moves(place, kvbuf, send_sem, recv_sem, dz, flip, half, tiles // 2)

    def hand_on(held, moves):
        for go, copy in moves:

            @pl.when(go & held)
            def _():
                copy.start()

    def arrived(source, half):
        piece = kvbuf.at[source, pl.ds(half * (tiles // 2), tiles // 2)]
        pltpu.make_async_copy(piece, piece, recv_sem.at[source, half]).wait()

    hand_steps = place.hand_order()

    def hand_one(c, carry):
        k = half = jnp.int32(0)
        for i, (_turn, block, part) in enumerate(hand_steps):
            k = jnp.where(c == i, block, k)
            half = jnp.where(c == i, part, half)
        source, held, moves = moves_of(k, half)

        @pl.when(held)
        def _():
            arrived(source, half)

        hand_on(held, moves)
        return carry

    for load in loads[2:5]:
        load.wait()

    wide = 256
    shift = CONV_DILATION
    tall = half_rows + edge

    def convolve(half, beside):
        at = half * half_rows
        parts = hidden // wide
        for p in range(parts):
            cols = slice(p * wide, (p + 1) * wide)
            low = jnp.dot(
                lifted[at : at + tall], taps[0, :, cols], preferred_element_type=jnp.float32
            )
            mid = jnp.dot(
                lifted[at + edge : at + edge + half_rows],
                taps[1, :, cols],
                preferred_element_type=jnp.float32,
            )
            high = jnp.dot(
                lifted[at + edge : at + edge + tall],
                taps[2, :, cols],
                preferred_element_type=jnp.float32,
            )
            for task in beside[p::parts]:
                task()
            conv = low[edge - shift : edge - shift + half_rows] + mid
            conv = conv + high[shift : shift + half_rows]
            squeezed[:, cols] = gelu(conv).astype(jnp.bfloat16)

    def project(half):
        at = half * half_rows
        here = slice(at, at + half_rows)
        square = jnp.zeros((half_rows, 128), jnp.float32)
        for n in range(0, channels, wide):
            part = act[here, n : n + wide].astype(jnp.float32) + jnp.dot(
                squeezed[...], mix[:, n : n + wide], preferred_element_type=jnp.float32
            )
            mixed[:, n : n + wide] = part
            for m in range(0, wide, 128):
                square = square + part[:, m : m + 128] * part[:, m : m + 128]
        mean = jnp.sum(square, axis=1, keepdims=True) * (1.0 / channels)
        factor = lax.rsqrt(mean + norm_eps)
        for n in range(0, channels, wide):
            normed[:, n : n + wide] = (mixed[:, n : n + wide] * factor).astype(jnp.bfloat16)
        keyval = jnp.dot(normed[...], wkv[...], preferred_element_type=jnp.float32)
        keys = keyval[:, :HDIM].astype(jnp.bfloat16)
        values = keyval[:, HDIM:].T.astype(jnp.bfloat16)
        for j in range(tiles // 2):
            cut = slice(j * tile, (j + 1) * tile)
            kvbuf[me, half * (tiles // 2) + j, :tile] = keys[cut]
            kvbuf[me, half * (tiles // 2) + j, tile:] = values[:, cut]
        _source, held, moves = moves_of(0, half)
        hand_on(held, moves)
        query = jnp.dot(normed[...], wq[...], preferred_element_type=jnp.float32)
        query = (query * (LOG2E / math.sqrt(HDIM))).T.astype(jnp.bfloat16)
        queries[:HDIM, here] = query

    beside = [
        functools.partial(lift, at, edge) for at in range(early_rows, rows, edge)
    ] + [functools.partial(turn_tile, code) for code in range(tiles_ref.shape[0])]
    convolve(0, beside)
    for load in loads[5:]:
        load.wait()
    project(0)
    lift_halo(1, has_next, to_prev)
    convolve(1, [])
    lax.fori_loop(0, place.near(), hand_one, 0)
    project(1)

    def absorb(source, special):
        delta = source - me
        keys = jnp.concatenate([kvbuf[source, j, :tile] for j in range(tiles)], axis=0)
        values = jnp.concatenate([kvbuf[source, j, tile:] for j in range(tiles)], axis=1)
        values = jnp.concatenate([values, jnp.ones((16, rows), jnp.bfloat16)], axis=0)
        lanes = tile
        line = [valid_ref[pl.ds(source * tiles + j, 1)] for j in range(tiles)]
        line = jnp.where(jnp.concatenate(line, axis=1) == 1, 0.0, masked_score)
        line = jnp.broadcast_to(line, (16, rows)).astype(jnp.bfloat16)
        mask = lax.dot_general(
            line,
            jnp.ones((16, lanes), jnp.bfloat16),
            (((0,), (0,)), ((), ())),
            preferred_element_type=jnp.float32,
        )
        if special:
            scores_buf[...] = jnp.dot(
                keys, queries[:HDIM], preferred_element_type=jnp.float32
            )
        else:
            keys = jnp.concatenate([keys, mask.astype(jnp.bfloat16)], axis=1)
            scores_buf[...] = jnp.dot(keys, queries[...], preferred_element_type=jnp.float32)
        shrinks = []
        for i in range(tiles):
            across = slice(i * tile, (i + 1) * tile)
            column = []
            for j in range(tiles):
                offset = jnp.clip(delta * tiles + (j - i) + offsets // 2, 0, offsets - 1)
                scores = scores_buf[j * tile : (j + 1) * tile, across] + table[codes_ref[i, offset]]
                if special:
                    key_row = lax.broadcasted_iota(jnp.int32, (tile, tile), 0) + j * tile
                    query_row = lax.broadcasted_iota(jnp.int32, (tile, tile), 1) + i * tile
                    apart = delta * rows + key_row - query_row
                    usable = mask[j * tile : (j + 1) * tile] >= 0.0
                    kept = (apart == 0) | ((jnp.abs(apart) <= HALF) & usable)
                    scores = jnp.where(kept, scores, masked_score)
                column.append(scores)
            column = jnp.concatenate(column, axis=0)
            old = peak[:, across]
            new = jnp.maximum(old, jnp.max(column, axis=0, keepdims=True))
            probs_buf[:, across] = jnp.exp2(column - new).astype(jnp.bfloat16)
            peak[:, across] = new
            shrinks.append(jnp.exp2(old - new))
        shrink = jnp.concatenate(shrinks, axis=1)
        weighted[...] = weighted[...] * shrink + jnp.dot(
            values, probs_buf[...], preferred_element_type=jnp.float32
        )

    def absorb_block(source):
        apart = jnp.abs(source - me)
        special = (apart == 0) | (apart == place.reach)

        @pl.when(special)
        def _():
            absorb(source, True)

        @pl.when(jnp.logical_not(special))
        def _():
            absorb(source, False)

    turns = 2 * place.steps

    def hand_one(c, carry):
        k = half = jnp.int32(0)
        for i, (_turn, block, part) in enumerate(hand_steps):
            k = jnp.where(c == i, block, k)
            half = jnp.where(c == i, part, half)
        source, held, moves = moves_of(k, half)

        @pl.when(held)
        def _():
            arrived(source, half)

        hand_on(held, moves)
        return carry

    def turn_of(u, done):
        until = jnp.int32(0)
        for turn, _block, _part in hand_steps:
            until = until + jnp.where(turn <= u, 1, 0)
        lax.fori_loop(done, until, hand_one, 0)
        dz, flip = place.step(u // 2)
        away = u % 2
        source_z = z + dz
        column = (y + flip) % 2 if columns == 2 else y
        source = place.index(source_z, column, (core + away) % 2)
        take = (source_z >= 0) & (source_z < place.planes) & place.needs(source, me)

        @pl.when(take)
        def _():
            @pl.when(away == 1)
            def _():
                arrived(source, 0)
                arrived(source, 1)

            absorb_block(source)

        return until

    lax.fori_loop(0, turns, turn_of, jnp.int32(place.near()))
    result = weighted[:HDIM] / weighted[HDIM : HDIM + 1]
    out_ref[...] = result.T.astype(out_ref.dtype)

    def drain(k, carry):
        for half in range(2):
            _source, _held, moves = moves_of(k, half)
            for go, copy in moves:

                @pl.when(go)
                def _():
                    copy.wait_send()

        return carry

    lax.fori_loop(0, place.steps, drain, 0)

    @pl.when(has_next)
    def _():
        to_next.wait_send()

    @pl.when(has_prev)
    def _():
        to_prev.wait_send()


def per_device(
    columns,
    activations,
    dilated_tap_weight,
    conv_mix,
    w_query,
    w_keyval,
    contact_tiles,
    tile_codes,
    bin_valid,
):
    rows, channels = activations.shape
    hidden = conv_mix.shape[0]
    half_rows = rows // 2
    edge = 16
    tile = contact_tiles.shape[1]
    count = lax.axis_size("seq")
    plane = 2 * columns
    far = -(-(HALF // rows) // plane)
    valid = bin_valid.reshape(count * rows // tile, tile)
    vmem = pl.BlockSpec(memory_space=pltpu.VMEM)
    smem = pl.BlockSpec(memory_space=pltpu.SMEM)
    hbm = pl.BlockSpec(memory_space=pl.ANY)
    bf16, f32 = jnp.bfloat16, jnp.float32
    return pl.pallas_call(
        functools.partial(layer_kernel, columns, count),
        out_shape=jax.ShapeDtypeStruct((rows, HDIM), bf16),
        in_specs=[hbm, hbm, hbm, hbm, hbm, vmem, smem, vmem],
        out_specs=vmem,
        scratch_shapes=[
            pltpu.VMEM(activations.shape, bf16),
            pltpu.VMEM(dilated_tap_weight.shape, bf16),
            pltpu.VMEM(conv_mix.shape, bf16),
            pltpu.VMEM(w_query.shape, bf16),
            pltpu.VMEM(w_keyval.shape, bf16),
            pltpu.VMEM((2, edge, channels), bf16),
            pltpu.VMEM((rows + 2 * edge, channels), bf16),
            pltpu.VMEM((half_rows, hidden), bf16),
            pltpu.VMEM((half_rows, channels), f32),
            pltpu.VMEM((half_rows, channels), bf16),
            pltpu.VMEM(contact_tiles.shape, f32),
            pltpu.VMEM((2 * HDIM, rows), bf16),
            pltpu.VMEM((rows, rows), f32),
            pltpu.VMEM((rows, rows), bf16),
            pltpu.VMEM((count, rows // tile, 2 * tile, HDIM), bf16),
            pltpu.VMEM((1, rows), f32),
            pltpu.VMEM((HDIM + 16, rows), f32),
            pltpu.SemaphoreType.DMA((8,)),
            pltpu.SemaphoreType.DMA((2,)),
            pltpu.SemaphoreType.DMA((2,)),
            pltpu.SemaphoreType.DMA((4, (2 * far + 1) * columns, 2)),
            pltpu.SemaphoreType.DMA((count, 2)),
        ],
        compiler_params=pltpu.CompilerParams(
            collective_id=0, has_side_effects=True, vmem_limit_bytes=56 * 1024 * 1024
        ),
        cost_estimate=pl.CostEstimate(
            flops=2 * rows * channels * (4 * hidden + 3 * HDIM) + 4 * rows * HDIM * 2 * HALF,
            bytes_accessed=14 * 1024 * 1024,
            transcendentals=rows * 2 * HALF,
        ),
    )(
        activations,
        dilated_tap_weight,
        conv_mix,
        w_query,
        w_keyval,
        contact_tiles,
        tile_codes,
        valid,
    )


def columns_of(mesh):
    along = mesh.devices.reshape(-1, mesh.shape["seq"])[0]
    first = along[0]
    if not hasattr(first, "coords"):
        return 2 if mesh.shape["seq"] == 16 else 1
    return sum(d.coords[2] == first.coords[2] for d in along) // 2


def solution(mesh):
    in_specs = (P(("grp", "seq"), None), P(), P(), P(), P(), P(), P(("grp", "seq"), None), P("grp"))
    out_specs = P(("grp", "seq"), None)
    return jax.shard_map(
        functools.partial(per_device, columns_of(mesh)),
        mesh=mesh,
        in_specs=in_specs,
        out_specs=out_specs,
        check_vma=False,
    )
```

```python
import functools
import math

import jax
import jax.numpy as jnp
from jax import lax
from jax.experimental import pallas as pl
from jax.experimental.pallas import tpu as pltpu
from jax.sharding import PartitionSpec as P

HDIM = 128
CONV_DILATION = 8
HALF = 4096
MESH = pl.DeviceIdType.MESH

masked_score = -1e30
norm_eps = 1e-06
LOG2E = math.log2(math.e)


class Place:
    def __init__(self, count, columns, reach):
        self.count = count
        self.columns = columns
        self.plane = 2 * columns
        self.planes = count // self.plane
        self.reach = reach
        self.far = -(-reach // self.plane)
        self.steps = (2 * self.far + 1) * columns
        me = lax.axis_index("seq")
        self.me = me
        self.z = me // self.plane
        self.y = (me % self.plane) // 2
        self.core = me % 2

    def index(self, z, y, core):
        return z * self.plane + y * 2 + core

    def order(self):
        blocks = [(0, 0)]
        late = [(0, 1)]
        for d in range(1, self.far + 1):
            if d == 1 and self.columns == 2:
                blocks += late
                late = []
            blocks += [(-d, 0), (d, 0)]
            if d > 1 and self.columns == 2:
                blocks += late
            late = [(-d, 1), (d, 1)]
        if self.columns == 2:
            blocks += late
        return blocks

    def hand_order(self):
        blocks = self.order()
        first = self.near()
        steps = [(0, k, 0) for k in range(1, first + 1)]
        steps += [(2, k, 1) for k in range(1, first + 1)]
        for k in range(first + 1, len(blocks), 2):
            early = 2 if self.columns == 2 and k == first + 1 else 0
            steps += [(2 * k - 2 - early, k, 0), (2 * k - 2 - early, k + 1, 0)]
            steps += [(2 * k - early, k, 1), (2 * k - early, k + 1, 1)]
        return steps

    def near(self):
        return 3 if self.columns == 2 else 2

    def step(self, k):
        dz = flip = jnp.int32(0)
        for i, (d, f) in enumerate(self.order()):
            dz = jnp.where(k == i, d, dz)
            flip = jnp.where(k == i, f, flip)
        return dz, flip

    def needs(self, source, target):
        return jnp.abs(source - target) <= self.reach


def block_moves(place, kvbuf, send_sem, recv_sem, dz, flip, half, part):
    z, y, core = place.z, place.y, place.core
    source_z = z + dz
    source = place.index(source_z, (y + flip) % 2 if place.columns == 2 else y, core)
    held = (source_z >= 0) & (source_z < place.planes) & place.needs(source, place.me)
    piece = kvbuf.at[source, pl.ds(half * part, part)]
    slot = (dz + place.far) * place.columns + flip
    edge = (source_z == 0) | (source_z == place.planes - 1)
    away = jnp.abs(dz)

    def along_z(distance):
        return (distance == 1) & (edge | (half == 1))

    def copy(kind, target):
        return pltpu.make_async_remote_copy(
            src_ref=piece,
            dst_ref=piece,
            send_sem=send_sem.at[kind, slot, half],
            recv_sem=recv_sem.at[source, half],
            device_id={"seq": target},
            device_id_type=MESH,
        )

    moves = []
    for kind, turn in ((0, 1), (1, -1)):
        target = jnp.clip(place.index(z + turn, y, core), 0, place.count - 1)
        go = held & (z + turn >= 0) & (z + turn < place.planes)
        go = go & (dz * turn <= 0) & (away + 1 <= place.far) & place.needs(source, target)
        go = go & ((flip == 0) | along_z(away + 1))
        moves.append((go, copy(kind, target)))
    if place.columns == 2:
        target = place.index(z, 1 - y, core)
        go = held & (flip == 0) & ((dz == 0) | jnp.logical_not(along_z(away)))
        moves.append((go & place.needs(source, target), copy(2, target)))
    target = place.index(z, y, 1 - core)
    moves.append((held & place.needs(source, target), copy(3, target)))
    return source, held, moves


def gelu(v):
    size = jnp.abs(v)
    low = 1.0 + (0.3275911 * math.sqrt(0.5)) * size
    t = pl.reciprocal(low, approx=True)
    t = t * (2.0 - low * t)
    poly = 0.5 * 1.061405429 * t - 0.5 * 1.453152027
    poly = poly * t + 0.5 * 1.421413741
    poly = poly * t - 0.5 * 0.284496736
    poly = (poly * t + 0.5 * 0.254829592) * t
    tail = poly * jnp.exp2((-0.5 * LOG2E) * (size * size))
    return jnp.maximum(v, 0.0) - size * tail


def layer_kernel(
    columns,
    count,
    act_hbm,
    taps_hbm,
    mix_hbm,
    wq_hbm,
    wkv_hbm,
    tiles_ref,
    codes_ref,
    valid_ref,
    out_ref,
    act,
    taps,
    mix,
    wq,
    wkv,
    halo,
    lifted,
    squeezed,
    mixed,
    normed,
    table,
    queries,
    mask,
    scores_buf,
    probs_buf,
    kvbuf,
    peak,
    weighted,
    load_sem,
    halo_send,
    halo_recv,
    send_sem,
    recv_sem,
):
    rows, channels = act.shape
    hidden = mix.shape[0]
    half_rows = rows // 2
    tile = table.shape[1]
    tiles = rows // tile
    offsets = codes_ref.shape[1]
    edge = halo.shape[1]
    early_rows = half_rows + 2 * edge
    place = Place(count, columns, HALF // rows)
    me, z, y, core = place.me, place.z, place.y, place.core

    wide = 256
    parts = hidden // wide
    loads = [
        pltpu.make_async_copy(
            act_hbm.at[pl.ds(0, early_rows)], act.at[pl.ds(0, early_rows)], load_sem.at[0]
        ),
        pltpu.make_async_copy(
            act_hbm.at[pl.ds(early_rows, rows - early_rows)],
            act.at[pl.ds(early_rows, rows - early_rows)],
            load_sem.at[1],
        ),
    ]
    tap_loads = []
    for p in range(parts):
        cols = pl.ds(p * wide, wide)
        tap_loads.append(
            pltpu.make_async_copy(taps_hbm.at[:, :, cols], taps.at[:, :, cols], load_sem.at[5 + p])
        )
    late_loads = [
        pltpu.make_async_copy(mix_hbm, mix, load_sem.at[2]),
        pltpu.make_async_copy(wkv_hbm, wkv, load_sem.at[3]),
        pltpu.make_async_copy(wq_hbm, wq, load_sem.at[4]),
    ]
    for load in loads:
        load.start()

    barrier = pltpu.get_barrier_semaphore()
    greeted = [(jnp.bool_(True), place.index(z, y, 1 - core))]
    if columns == 2:
        greeted.append((jnp.bool_(True), place.index(z, 1 - y, core)))
    for turn in (1, -1):
        ok = (z + turn >= 0) & (z + turn < place.planes)
        greeted.append((ok, jnp.clip(place.index(z + turn, y, core), 0, count - 1)))
    beyond = me + 2 * core - 1
    greeted.append(((beyond >= 0) & (beyond < count), jnp.clip(beyond, 0, count - 1)))
    for ok, target in greeted:

        @pl.when(ok)
        def _():
            pl.semaphore_signal(barrier, inc=1, device_id={"seq": target}, device_id_type=MESH)

    loads[0].wait()
    for load in tap_loads + late_loads:
        load.start()
    loads[1].wait()
    pl.semaphore_wait(barrier, sum(ok.astype(jnp.int32) for ok, _target in greeted))

    has_next = me + 1 < count
    has_prev = me > 0
    to_next = pltpu.make_async_remote_copy(
        src_ref=act.at[pl.ds(rows - edge, edge)],
        dst_ref=halo.at[0],
        send_sem=halo_send.at[0],
        recv_sem=halo_recv.at[0],
        device_id={"seq": jnp.minimum(me + 1, count - 1)},
        device_id_type=MESH,
    )
    to_prev = pltpu.make_async_remote_copy(
        src_ref=act.at[pl.ds(0, edge)],
        dst_ref=halo.at[1],
        send_sem=halo_send.at[1],
        recv_sem=halo_recv.at[1],
        device_id={"seq": jnp.maximum(me - 1, 0)},
        device_id_type=MESH,
    )

    @pl.when(has_next)
    def _():
        to_next.start()

    @pl.when(has_prev)
    def _():
        to_prev.start()

    peak[...] = jnp.full(peak.shape, masked_score, jnp.float32)
    spare = lax.broadcasted_iota(jnp.int32, (HDIM, rows), 0) == 0
    queries[HDIM:] = jnp.where(spare, 1.0, 0.0).astype(jnp.bfloat16)
    weighted[...] = jnp.zeros(weighted.shape, jnp.float32)

    def lift(at, count):
        raised = gelu(act[pl.ds(at, count)].astype(jnp.float32))
        lifted[pl.ds(at + edge, count)] = raised.astype(jnp.bfloat16)

    def lift_strip(strip, carry):
        lift(pl.multiple_of(strip * 2 * edge, 2 * edge), 2 * edge)
        return carry

    def turn_tile(code):
        table[code] = tiles_ref[code].astype(jnp.float32).T * LOG2E

    lax.fori_loop(0, early_rows // (2 * edge), lift_strip, 0)

    def lift_halo(side, there, copy):
        at = side * (rows + edge)

        @pl.when(there)
        def _():
            copy.wait_recv()
            lifted[at : at + edge] = gelu(halo[side].astype(jnp.float32)).astype(jnp.bfloat16)

        @pl.when(jnp.logical_not(there))
        def _():
            lifted[at : at + edge] = jnp.zeros((edge, channels), jnp.bfloat16)

    for code in range(tiles_ref.shape[0]):
        turn_tile(code)

    def mask_of(d, carry):
        source = me + d - place.reach

        @pl.when((source >= 0) & (source < count))
        def _():
            line = [valid_ref[pl.ds(source * tiles + j, 1)] for j in range(tiles)]
            line = jnp.where(jnp.concatenate(line, axis=1) == 1, 0.0, masked_score)
            line = jnp.broadcast_to(line, (16, rows)).astype(jnp.bfloat16)
            spread = lax.dot_general(
                line,
                jnp.ones((16, HDIM), jnp.bfloat16),
                (((0,), (0,)), ((), ())),
                preferred_element_type=jnp.float32,
            )
            mask[source] = spread.astype(jnp.bfloat16)

        return carry

    lax.fori_loop(0, 2 * place.reach + 1, mask_of, 0)
    lift_halo(0, has_prev, to_next)
    lift_halo(1, has_next, to_prev)

    def moves_of(k, half):
        dz, flip = place.step(k)
        return block_moves(place, kvbuf, send_sem, recv_sem, dz, flip, half, tiles // 2)

    def hand_on(held, moves):
        for go, copy in moves:

            @pl.when(go & held)
            def _():
                copy.start()

    def arrived(source, half):
        piece = kvbuf.at[source, pl.ds(half * (tiles // 2), tiles // 2)]
        pltpu.make_async_copy(piece, piece, recv_sem.at[source, half]).wait()

    hand_steps = place.hand_order()

    def hand_one(c, carry):
        k = half = jnp.int32(0)
        for i, (_turn, block, part) in enumerate(hand_steps):
            k = jnp.where(c == i, block, k)
            half = jnp.where(c == i, part, half)
        source, held, moves = moves_of(k, half)

        @pl.when(held)
        def _():
            arrived(source, half)

        hand_on(held, moves)
        return carry

    shift = CONV_DILATION
    tall = half_rows + edge

    def convolve(half, beside):
        at = half * half_rows
        for p in range(parts):
            cols = slice(p * wide, (p + 1) * wide)
            if half == 0:
                tap_loads[p].wait()
            low = jnp.dot(
                lifted[at : at + tall], taps[0, :, cols], preferred_element_type=jnp.float32
            )
            mid = jnp.dot(
                lifted[at + edge : at + edge + half_rows],
                taps[1, :, cols],
                preferred_element_type=jnp.float32,
            )
            high = jnp.dot(
                lifted[at + edge : at + edge + tall],
                taps[2, :, cols],
                preferred_element_type=jnp.float32,
            )
            for task in beside[p::parts]:
                task()
            conv = low[edge - shift : edge - shift + half_rows] + mid
            conv = conv + high[shift : shift + half_rows]
            squeezed[:, cols] = gelu(conv).astype(jnp.bfloat16)

    def project(half):
        at = half * half_rows
        here = slice(at, at + half_rows)
        square = jnp.zeros((half_rows, 128), jnp.float32)
        for n in range(0, channels, wide):
            part = act[here, n : n + wide].astype(jnp.float32) + jnp.dot(
                squeezed[...], mix[:, n : n + wide], preferred_element_type=jnp.float32
            )
            mixed[:, n : n + wide] = part
            for m in range(0, wide, 128):
                square = square + part[:, m : m + 128] * part[:, m : m + 128]
        mean = jnp.sum(square, axis=1, keepdims=True) * (1.0 / channels)
        factor = lax.rsqrt(mean + norm_eps)
        for n in range(0, channels, wide):
            normed[:, n : n + wide] = (mixed[:, n : n + wide] * factor).astype(jnp.bfloat16)
        keyval = jnp.dot(normed[...], wkv[...], preferred_element_type=jnp.float32)
        keys = keyval[:, :HDIM].astype(jnp.bfloat16)
        values = keyval[:, HDIM:].T.astype(jnp.bfloat16)
        for j in range(tiles // 2):
            cut = slice(j * tile, (j + 1) * tile)
            kvbuf[me, half * (tiles // 2) + j, :tile] = keys[cut]
            kvbuf[me, half * (tiles // 2) + j, tile:] = values[:, cut]
        _source, held, moves = moves_of(0, half)
        hand_on(held, moves)
        query = jnp.dot(normed[...], wq[...], preferred_element_type=jnp.float32)
        query = (query * (LOG2E / math.sqrt(HDIM))).T.astype(jnp.bfloat16)
        queries[:HDIM, here] = query

    beside = [functools.partial(lift, at, edge) for at in range(early_rows, rows, edge)]
    convolve(0, beside)
    for load in late_loads:
        load.wait()
    project(0)
    convolve(1, [])
    lax.fori_loop(0, place.near(), hand_one, 0)
    project(1)

    def absorb(source, special):
        delta = source - me
        keys = jnp.concatenate([kvbuf[source, j, :tile] for j in range(tiles)], axis=0)
        values = jnp.concatenate([kvbuf[source, j, tile:] for j in range(tiles)], axis=1)
        values = jnp.concatenate([values, jnp.ones((16, rows), jnp.bfloat16)], axis=0)
        if special:
            looked = queries.at[:HDIM]
        else:
            keys = jnp.concatenate([keys, mask[source]], axis=1)
            looked = queries
        spans = [slice(n, n + 2 * tile) for n in range(0, rows, 2 * tile)]
        for span in spans:
            scores_buf[:, span] = jnp.dot(
                keys, looked[:, span], preferred_element_type=jnp.float32
            )
        for span in spans:
            shrinks = []
            for i in range(span.start // tile, span.stop // tile):
                across = slice(i * tile, (i + 1) * tile)
                column = []
                highs = []
                for j in range(tiles):
                    down = slice(j * tile, (j + 1) * tile)
                    offset = jnp.clip(delta * tiles + (j - i) + offsets // 2, 0, offsets - 1)
                    scores = scores_buf[down, across] + table[codes_ref[i, offset]]
                    if special:
                        key_row = lax.broadcasted_iota(jnp.int32, (tile, tile), 0) + j * tile
                        query_row = lax.broadcasted_iota(jnp.int32, (tile, tile), 1) + i * tile
                        apart = delta * rows + key_row - query_row
                        usable = mask[source, down].astype(jnp.float32) >= 0.0
                        kept = (apart == 0) | ((jnp.abs(apart) <= HALF) & usable)
                        scores = jnp.where(kept, scores, masked_score)
                    column.append(scores)
                    highs.append(jnp.max(scores.reshape(tile // 8, 8, tile), axis=0))
                while len(highs) > 1:
                    highs = [jnp.maximum(u, v) for u, v in zip(highs[::2], highs[1::2])]
                old = peak[:, across]
                new = jnp.maximum(old, jnp.max(highs[0], axis=0, keepdims=True))
                for j in range(tiles):
                    probs_buf[j * tile : (j + 1) * tile, across] = jnp.exp2(
                        column[j] - new
                    ).astype(jnp.bfloat16)
                peak[:, across] = new
                shrinks.append(jnp.exp2(old - new))
            shrink = jnp.concatenate(shrinks, axis=1)
            weighted[:, span] = weighted[:, span] * shrink + jnp.dot(
                values, probs_buf[:, span], preferred_element_type=jnp.float32
            )

    def absorb_block(source):
        apart = jnp.abs(source - me)
        special = (apart == 0) | (apart == place.reach)

        @pl.when(special)
        def _():
            absorb(source, True)

        @pl.when(jnp.logical_not(special))
        def _():
            absorb(source, False)

    turns = 2 * place.steps

    def hand_one(c, carry):
        k = half = jnp.int32(0)
        for i, (_turn, block, part) in enumerate(hand_steps):
            k = jnp.where(c == i, block, k)
            half = jnp.where(c == i, part, half)
        source, held, moves = moves_of(k, half)

        @pl.when(held)
        def _():
            arrived(source, half)

        hand_on(held, moves)
        return carry

    def turn_of(u, done):
        until = jnp.int32(0)
        for turn, _block, _part in hand_steps:
            until = until + jnp.where(turn <= u, 1, 0)
        lax.fori_loop(done, until, hand_one, 0)
        dz, flip = place.step(u // 2)
        away = u % 2
        source_z = z + dz
        column = (y + flip) % 2 if columns == 2 else y
        source = place.index(source_z, column, (core + away) % 2)
        take = (source_z >= 0) & (source_z < place.planes) & place.needs(source, me)

        @pl.when(take)
        def _():
            @pl.when(away == 1)
            def _():
                arrived(source, 0)
                arrived(source, 1)

            absorb_block(source)

        return until

    lax.fori_loop(0, turns, turn_of, jnp.int32(place.near()))
    result = weighted[:HDIM] / weighted[HDIM : HDIM + 1]
    out_ref[...] = result.T.astype(out_ref.dtype)

    def drain(k, carry):
        for half in range(2):
            _source, _held, moves = moves_of(k, half)
            for go, copy in moves:

                @pl.when(go)
                def _():
                    copy.wait_send()

        return carry

    lax.fori_loop(0, place.steps, drain, 0)

    @pl.when(has_next)
    def _():
        to_next.wait_send()

    @pl.when(has_prev)
    def _():
        to_prev.wait_send()


def per_device(
    columns,
    activations,
    dilated_tap_weight,
    conv_mix,
    w_query,
    w_keyval,
    contact_tiles,
    tile_codes,
    bin_valid,
):
    rows, channels = activations.shape
    hidden = conv_mix.shape[0]
    half_rows = rows // 2
    edge = 16
    tile = contact_tiles.shape[1]
    count = lax.axis_size("seq")
    plane = 2 * columns
    far = -(-(HALF // rows) // plane)
    valid = bin_valid.reshape(count * rows // tile, tile)
    vmem = pl.BlockSpec(memory_space=pltpu.VMEM)
    smem = pl.BlockSpec(memory_space=pltpu.SMEM)
    hbm = pl.BlockSpec(memory_space=pl.ANY)
    bf16, f32 = jnp.bfloat16, jnp.float32
    return pl.pallas_call(
        functools.partial(layer_kernel, columns, count),
        out_shape=jax.ShapeDtypeStruct((rows, HDIM), bf16),
        in_specs=[hbm, hbm, hbm, hbm, hbm, vmem, smem, vmem],
        out_specs=vmem,
        scratch_shapes=[
            pltpu.VMEM(activations.shape, bf16),
            pltpu.VMEM(dilated_tap_weight.shape, bf16),
            pltpu.VMEM(conv_mix.shape, bf16),
            pltpu.VMEM(w_query.shape, bf16),
            pltpu.VMEM(w_keyval.shape, bf16),
            pltpu.VMEM((2, edge, channels), bf16),
            pltpu.VMEM((rows + 2 * edge, channels), bf16),
            pltpu.VMEM((half_rows, hidden), bf16),
            pltpu.VMEM((half_rows, channels), f32),
            pltpu.VMEM((half_rows, channels), bf16),
            pltpu.VMEM(contact_tiles.shape, f32),
            pltpu.VMEM((2 * HDIM, rows), bf16),
            pltpu.VMEM((count, rows, HDIM), bf16),
            pltpu.VMEM((rows, rows), f32),
            pltpu.VMEM((rows, rows), bf16),
            pltpu.VMEM((count, rows // tile, 2 * tile, HDIM), bf16),
            pltpu.VMEM((1, rows), f32),
            pltpu.VMEM((HDIM + 16, rows), f32),
            pltpu.SemaphoreType.DMA((5 + hidden // 256,)),
            pltpu.SemaphoreType.DMA((2,)),
            pltpu.SemaphoreType.DMA((2,)),
            pltpu.SemaphoreType.DMA((4, (2 * far + 1) * columns, 2)),
            pltpu.SemaphoreType.DMA((count, 2)),
        ],
        compiler_params=pltpu.CompilerParams(
            collective_id=0, has_side_effects=True, vmem_limit_bytes=56 * 1024 * 1024
        ),
        cost_estimate=pl.CostEstimate(
            flops=2 * rows * channels * (4 * hidden + 3 * HDIM) + 4 * rows * HDIM * 2 * HALF,
            bytes_accessed=14 * 1024 * 1024,
            transcendentals=rows * 2 * HALF,
        ),
    )(
        activations,
        dilated_tap_weight,
        conv_mix,
        w_query,
        w_keyval,
        contact_tiles,
        tile_codes,
        valid,
    )


def columns_of(mesh):
    along = mesh.devices.reshape(-1, mesh.shape["seq"])[0]
    first = along[0]
    if not hasattr(first, "coords"):
        return 2 if mesh.shape["seq"] == 16 else 1
    return sum(d.coords[2] == first.coords[2] for d in along) // 2


def solution(mesh):
    in_specs = (P(("grp", "seq"), None), P(), P(), P(), P(), P(), P(("grp", "seq"), None), P("grp"))
    out_specs = P(("grp", "seq"), None)
    return jax.shard_map(
        functools.partial(per_device, columns_of(mesh)),
        mesh=mesh,
        in_specs=in_specs,
        out_specs=out_specs,
        check_vma=False,
    )
```

```python
import functools
import math

import jax
import jax.numpy as jnp
from jax import lax
from jax.experimental import pallas as pl
from jax.experimental.pallas import tpu as pltpu
from jax.sharding import PartitionSpec as P

HDIM = 128
CONV_DILATION = 8
HALF = 4096
MESH = pl.DeviceIdType.MESH

masked_score = -1e30
norm_eps = 1e-06
LOG2E = math.log2(math.e)


class Place:
    def __init__(self, count, columns, reach):
        self.count = count
        self.columns = columns
        self.plane = 2 * columns
        self.planes = count // self.plane
        self.reach = reach
        self.far = -(-reach // self.plane)
        self.steps = (2 * self.far + 1) * columns
        me = lax.axis_index("seq")
        self.me = me
        self.z = me // self.plane
        self.y = (me % self.plane) // 2
        self.core = me % 2

    def index(self, z, y, core):
        return z * self.plane + y * 2 + core

    def order(self):
        blocks = [(0, 0)]
        late = [(0, 1)]
        for d in range(1, self.far + 1):
            if d == 1 and self.columns == 2:
                blocks += late
                late = []
            blocks += [(-d, 0), (d, 0)]
            if d > 1 and self.columns == 2:
                blocks += late
            late = [(-d, 1), (d, 1)]
        if self.columns == 2:
            blocks += late
        return blocks

    def hand_order(self):
        blocks = self.order()
        first = self.near()
        steps = [(0, k, 0) for k in range(1, first + 1)]
        steps += [(2, k, 1) for k in range(1, first + 1)]
        for k in range(first + 1, len(blocks), 2):
            early = 2 if self.columns == 2 and k == first + 1 else 0
            steps += [(2 * k - 2 - early, k, 0), (2 * k - 2 - early, k + 1, 0)]
            steps += [(2 * k - early, k, 1), (2 * k - early, k + 1, 1)]
        return steps

    def near(self):
        return 3 if self.columns == 2 else 2

    def step(self, k):
        dz = flip = jnp.int32(0)
        for i, (d, f) in enumerate(self.order()):
            dz = jnp.where(k == i, d, dz)
            flip = jnp.where(k == i, f, flip)
        return dz, flip

    def needs(self, source, target):
        return jnp.abs(source - target) <= self.reach


def block_moves(place, kvbuf, send_sem, recv_sem, dz, flip, half, part):
    z, y, core = place.z, place.y, place.core
    source_z = z + dz
    source = place.index(source_z, (y + flip) % 2 if place.columns == 2 else y, core)
    held = (source_z >= 0) & (source_z < place.planes) & place.needs(source, place.me)
    piece = kvbuf.at[source, pl.ds(half * part, part)]
    slot = (dz + place.far) * place.columns + flip
    edge = (source_z == 0) | (source_z == place.planes - 1)
    away = jnp.abs(dz)

    def along_z(distance):
        return (distance == 1) & (edge | (half == 1))

    def copy(kind, target):
        return pltpu.make_async_remote_copy(
            src_ref=piece,
            dst_ref=piece,
            send_sem=send_sem.at[kind, slot, half],
            recv_sem=recv_sem.at[source, half],
            device_id={"seq": target},
            device_id_type=MESH,
        )

    moves = []
    for kind, turn in ((0, 1), (1, -1)):
        target = jnp.clip(place.index(z + turn, y, core), 0, place.count - 1)
        go = held & (z + turn >= 0) & (z + turn < place.planes)
        go = go & (dz * turn <= 0) & (away + 1 <= place.far) & place.needs(source, target)
        go = go & ((flip == 0) | along_z(away + 1))
        moves.append((go, copy(kind, target)))
    if place.columns == 2:
        target = place.index(z, 1 - y, core)
        go = held & (flip == 0) & ((dz == 0) | jnp.logical_not(along_z(away)))
        moves.append((go & place.needs(source, target), copy(2, target)))
    target = place.index(z, y, 1 - core)
    moves.append((held & place.needs(source, target), copy(3, target)))
    return source, held, moves


def gelu(v):
    size = jnp.abs(v)
    low = 1.0 + (0.3275911 * math.sqrt(0.5)) * size
    t = pl.reciprocal(low, approx=True)
    t = t * (2.0 - low * t)
    poly = 0.5 * 1.061405429 * t - 0.5 * 1.453152027
    poly = poly * t + 0.5 * 1.421413741
    poly = poly * t - 0.5 * 0.284496736
    poly = (poly * t + 0.5 * 0.254829592) * t
    tail = poly * jnp.exp2((-0.5 * LOG2E) * (size * size))
    return jnp.maximum(v, 0.0) - size * tail


def layer_kernel(
    columns,
    count,
    act_hbm,
    taps_hbm,
    mix_hbm,
    wq_hbm,
    wkv_hbm,
    tiles_hbm,
    codes_hbm,
    valid_hbm,
    out_ref,
    tiles_ref,
    codes_ref,
    valid_ref,
    act,
    taps,
    mix,
    wq,
    wkv,
    halo,
    lifted,
    squeezed,
    mixed,
    normed,
    table,
    queries,
    scores_buf,
    probs_buf,
    kvbuf,
    peak,
    weighted,
    load_sem,
    halo_send,
    halo_recv,
    send_sem,
    recv_sem,
):
    rows, channels = act.shape
    hidden = mix.shape[0]
    half_rows = rows // 2
    tile = table.shape[1]
    tiles = rows // tile
    offsets = codes_ref.shape[1]
    edge = halo.shape[1]
    early_rows = half_rows + 2 * edge
    place = Place(count, columns, HALF // rows)
    me, z, y, core = place.me, place.z, place.y, place.core

    wide = 256
    parts = hidden // wide
    loads = [
        pltpu.make_async_copy(
            act_hbm.at[pl.ds(0, early_rows)], act.at[pl.ds(0, early_rows)], load_sem.at[0]
        ),
        pltpu.make_async_copy(
            act_hbm.at[pl.ds(early_rows, rows - early_rows)],
            act.at[pl.ds(early_rows, rows - early_rows)],
            load_sem.at[1],
        ),
    ]
    tap_loads = [
        pltpu.make_async_copy(taps_hbm.at[tap], taps.at[tap], load_sem.at[5 + tap])
        for tap in range(3)
    ]
    late_loads = [
        pltpu.make_async_copy(mix_hbm, mix, load_sem.at[2]),
        pltpu.make_async_copy(wkv_hbm, wkv, load_sem.at[3]),
        pltpu.make_async_copy(wq_hbm, wq, load_sem.at[4]),
    ]
    small_loads = [
        pltpu.make_async_copy(tiles_hbm, tiles_ref, load_sem.at[8]),
        pltpu.make_async_copy(codes_hbm, codes_ref, load_sem.at[9]),
        pltpu.make_async_copy(valid_hbm, valid_ref, load_sem.at[10]),
    ]
    for load in loads + tap_loads + late_loads + small_loads:
        load.start()

    barrier = pltpu.get_barrier_semaphore()
    greeted = [(jnp.bool_(True), place.index(z, y, 1 - core))]
    if columns == 2:
        greeted.append((jnp.bool_(True), place.index(z, 1 - y, core)))
    for turn in (1, -1):
        ok = (z + turn >= 0) & (z + turn < place.planes)
        greeted.append((ok, jnp.clip(place.index(z + turn, y, core), 0, count - 1)))
    beyond = me + 2 * core - 1
    greeted.append(((beyond >= 0) & (beyond < count), jnp.clip(beyond, 0, count - 1)))
    for ok, target in greeted:

        @pl.when(ok)
        def _():
            pl.semaphore_signal(barrier, inc=1, device_id={"seq": target}, device_id_type=MESH)

    loads[0].wait()
    loads[1].wait()
    pl.semaphore_wait(barrier, sum(ok.astype(jnp.int32) for ok, _target in greeted))

    has_next = me + 1 < count
    has_prev = me > 0
    to_next = pltpu.make_async_remote_copy(
        src_ref=act.at[pl.ds(rows - edge, edge)],
        dst_ref=halo.at[0],
        send_sem=halo_send.at[0],
        recv_sem=halo_recv.at[0],
        device_id={"seq": jnp.minimum(me + 1, count - 1)},
        device_id_type=MESH,
    )
    to_prev = pltpu.make_async_remote_copy(
        src_ref=act.at[pl.ds(0, edge)],
        dst_ref=halo.at[1],
        send_sem=halo_send.at[1],
        recv_sem=halo_recv.at[1],
        device_id={"seq": jnp.maximum(me - 1, 0)},
        device_id_type=MESH,
    )

    @pl.when(has_next)
    def _():
        to_next.start()

    @pl.when(has_prev)
    def _():
        to_prev.start()

    peak[...] = jnp.full(peak.shape, masked_score, jnp.float32)
    spare = lax.broadcasted_iota(jnp.int32, (HDIM, rows), 0) == 0
    queries[HDIM:] = jnp.where(spare, 1.0, 0.0).astype(jnp.bfloat16)
    weighted[...] = jnp.zeros(weighted.shape, jnp.float32)

    def lift(at, count):
        raised = gelu(act[pl.ds(at, count)].astype(jnp.float32))
        lifted[pl.ds(at + edge, count)] = raised.astype(jnp.bfloat16)

    def lift_strip(strip, carry):
        lift(pl.multiple_of(strip * 2 * edge, 2 * edge), 2 * edge)
        return carry

    def turn_tile(code):
        table[code] = tiles_ref[code].T.astype(jnp.float32) * LOG2E

    lax.fori_loop(0, early_rows // (2 * edge), lift_strip, 0)

    def lift_halo(side, there, copy):
        at = side * (rows + edge)

        @pl.when(there)
        def _():
            copy.wait_recv()
            lifted[at : at + edge] = gelu(halo[side].astype(jnp.float32)).astype(jnp.bfloat16)

        @pl.when(jnp.logical_not(there))
        def _():
            lifted[at : at + edge] = jnp.zeros((edge, channels), jnp.bfloat16)

    lift_halo(0, has_prev, to_next)
    lift_halo(1, has_next, to_prev)

    def moves_of(k, half):
        dz, flip = place.step(k)
        return block_moves(place, kvbuf, send_sem, recv_sem, dz, flip, half, tiles // 2)

    def hand_on(held, moves):
        for go, copy in moves:

            @pl.when(go & held)
            def _():
                copy.start()

    def arrived(source, half):
        piece = kvbuf.at[source, pl.ds(half * (tiles // 2), tiles // 2)]
        pltpu.make_async_copy(piece, piece, recv_sem.at[source, half]).wait()

    hand_steps = place.hand_order()

    def hand_one(c, carry):
        k = half = jnp.int32(0)
        for i, (_turn, block, part) in enumerate(hand_steps):
            k = jnp.where(c == i, block, k)
            half = jnp.where(c == i, part, half)
        source, held, moves = moves_of(k, half)

        @pl.when(held)
        def _():
            arrived(source, half)

        hand_on(held, moves)
        return carry

    shift = CONV_DILATION
    tall = half_rows + edge

    def convolve(half, beside):
        at = half * half_rows
        for p in range(parts):
            cols = slice(p * wide, (p + 1) * wide)
            low = jnp.dot(
                lifted[at : at + tall], taps[0, :, cols], preferred_element_type=jnp.float32
            )
            mid = jnp.dot(
                lifted[at + edge : at + edge + half_rows],
                taps[1, :, cols],
                preferred_element_type=jnp.float32,
            )
            high = jnp.dot(
                lifted[at + edge : at + edge + tall],
                taps[2, :, cols],
                preferred_element_type=jnp.float32,
            )
            for task in beside[p::parts]:
                task()
            conv = low[edge - shift : edge - shift + half_rows] + mid
            conv = conv + high[shift : shift + half_rows]
            squeezed[:, cols] = gelu(conv).astype(jnp.bfloat16)

    def project(half):
        at = half * half_rows
        here = slice(at, at + half_rows)
        square = jnp.zeros((half_rows, 128), jnp.float32)
        for n in range(0, channels, wide):
            part = act[here, n : n + wide].astype(jnp.float32) + jnp.dot(
                squeezed[...], mix[:, n : n + wide], preferred_element_type=jnp.float32
            )
            mixed[:, n : n + wide] = part
            for m in range(0, wide, 128):
                square = square + part[:, m : m + 128] * part[:, m : m + 128]
        mean = jnp.sum(square, axis=1, keepdims=True) * (1.0 / channels)
        factor = lax.rsqrt(mean + norm_eps)
        for n in range(0, channels, wide):
            normed[:, n : n + wide] = (mixed[:, n : n + wide] * factor).astype(jnp.bfloat16)
        keyval = jnp.dot(normed[...], wkv[...], preferred_element_type=jnp.float32)
        keys = keyval[:, :HDIM].astype(jnp.bfloat16)
        values = keyval[:, HDIM:].T.astype(jnp.bfloat16)
        for j in range(tiles // 2):
            cut = slice(j * tile, (j + 1) * tile)
            kvbuf[me, half * (tiles // 2) + j, :tile] = keys[cut]
            kvbuf[me, half * (tiles // 2) + j, tile:] = values[:, cut]
        _source, held, moves = moves_of(0, half)
        hand_on(held, moves)
        query = jnp.dot(normed[...], wq[...], preferred_element_type=jnp.float32)
        query = (query * (LOG2E / math.sqrt(HDIM))).T.astype(jnp.bfloat16)
        queries[:HDIM, here] = query

    beside = [functools.partial(lift, at, edge) for at in range(early_rows, rows, edge)]
    for load in tap_loads:
        load.wait()
    convolve(0, beside)
    for load in late_loads:
        load.wait()
    project(0)
    convolve(1, [])
    lax.fori_loop(0, place.near(), hand_one, 0)
    project(1)
    for load in small_loads:
        load.wait()
    for code in range(tiles_ref.shape[0]):
        turn_tile(code)

    def absorb(source, special):
        delta = source - me
        keys = jnp.concatenate([kvbuf[source, j, :tile] for j in range(tiles)], axis=0)
        values = jnp.concatenate([kvbuf[source, j, tile:] for j in range(tiles)], axis=1)
        values = jnp.concatenate([values, jnp.ones((16, rows), jnp.bfloat16)], axis=0)
        line = [valid_ref[pl.ds(source * tiles + j, 1)] for j in range(tiles)]
        line = jnp.where(jnp.concatenate(line, axis=1) == 1, 0.0, masked_score)
        line = jnp.broadcast_to(line, (16, rows)).astype(jnp.bfloat16)
        mask = lax.dot_general(
            line,
            jnp.ones((16, HDIM), jnp.bfloat16),
            (((0,), (0,)), ((), ())),
            preferred_element_type=jnp.float32,
        )
        if special:
            looked = queries.at[:HDIM]
        else:
            keys = jnp.concatenate([keys, mask.astype(jnp.bfloat16)], axis=1)
            looked = queries
        spans = [slice(n, n + 2 * tile) for n in range(0, rows, 2 * tile)]
        for span in spans:
            scores_buf[:, span] = jnp.dot(
                keys, looked[:, span], preferred_element_type=jnp.float32
            )
        for span in spans:
            shrinks = []
            for i in range(span.start // tile, span.stop // tile):
                across = slice(i * tile, (i + 1) * tile)
                column = []
                highs = []
                for j in range(tiles):
                    down = slice(j * tile, (j + 1) * tile)
                    offset = jnp.clip(delta * tiles + (j - i) + offsets // 2, 0, offsets - 1)
                    scores = scores_buf[down, across] + table[codes_ref[i, offset]]
                    if special:
                        key_row = lax.broadcasted_iota(jnp.int32, (tile, tile), 0) + j * tile
                        query_row = lax.broadcasted_iota(jnp.int32, (tile, tile), 1) + i * tile
                        apart = delta * rows + key_row - query_row
                        usable = mask[down] >= 0.0
                        kept = (apart == 0) | ((jnp.abs(apart) <= HALF) & usable)
                        scores = jnp.where(kept, scores, masked_score)
                    column.append(scores)
                    highs.append(jnp.max(scores.reshape(tile // 8, 8, tile), axis=0))
                while len(highs) > 1:
                    highs = [jnp.maximum(u, v) for u, v in zip(highs[::2], highs[1::2])]
                old = peak[:, across]
                new = jnp.maximum(old, jnp.max(highs[0], axis=0, keepdims=True))
                for j in range(tiles):
                    probs_buf[j * tile : (j + 1) * tile, across] = jnp.exp2(
                        column[j] - new
                    ).astype(jnp.bfloat16)
                peak[:, across] = new
                shrinks.append(jnp.exp2(old - new))
            shrink = jnp.concatenate(shrinks, axis=1)
            weighted[:, span] = weighted[:, span] * shrink + jnp.dot(
                values, probs_buf[:, span], preferred_element_type=jnp.float32
            )

    def absorb_block(source):
        apart = jnp.abs(source - me)
        special = (apart == 0) | (apart == place.reach)

        @pl.when(special)
        def _():
            absorb(source, True)

        @pl.when(jnp.logical_not(special))
        def _():
            absorb(source, False)

    turns = 2 * place.steps

    def hand_one(c, carry):
        k = half = jnp.int32(0)
        for i, (_turn, block, part) in enumerate(hand_steps):
            k = jnp.where(c == i, block, k)
            half = jnp.where(c == i, part, half)
        source, held, moves = moves_of(k, half)

        @pl.when(held)
        def _():
            arrived(source, half)

        hand_on(held, moves)
        return carry

    def turn_of(u, done):
        until = jnp.int32(0)
        for turn, _block, _part in hand_steps:
            until = until + jnp.where(turn <= u, 1, 0)
        lax.fori_loop(done, until, hand_one, 0)
        dz, flip = place.step(u // 2)
        away = u % 2
        source_z = z + dz
        column = (y + flip) % 2 if columns == 2 else y
        source = place.index(source_z, column, (core + away) % 2)
        take = (source_z >= 0) & (source_z < place.planes) & place.needs(source, me)

        @pl.when(take)
        def _():
            @pl.when(away == 1)
            def _():
                arrived(source, 0)
                arrived(source, 1)

            absorb_block(source)

        return until

    lax.fori_loop(0, turns, turn_of, jnp.int32(place.near()))
    result = weighted[:HDIM] / weighted[HDIM : HDIM + 1]
    out_ref[...] = result.T.astype(out_ref.dtype)

    def drain(k, carry):
        for half in range(2):
            _source, _held, moves = moves_of(k, half)
            for go, copy in moves:

                @pl.when(go)
                def _():
                    copy.wait_send()

        return carry

    lax.fori_loop(0, place.steps, drain, 0)

    @pl.when(has_next)
    def _():
        to_next.wait_send()

    @pl.when(has_prev)
    def _():
        to_prev.wait_send()


def per_device(
    columns,
    activations,
    dilated_tap_weight,
    conv_mix,
    w_query,
    w_keyval,
    contact_tiles,
    tile_codes,
    bin_valid,
):
    rows, channels = activations.shape
    hidden = conv_mix.shape[0]
    half_rows = rows // 2
    edge = 16
    tile = contact_tiles.shape[1]
    count = lax.axis_size("seq")
    plane = 2 * columns
    far = -(-(HALF // rows) // plane)
    valid = bin_valid.reshape(count * rows // tile, tile)
    vmem = pl.BlockSpec(memory_space=pltpu.VMEM)
    hbm = pl.BlockSpec(memory_space=pl.ANY)
    bf16, f32 = jnp.bfloat16, jnp.float32
    return pl.pallas_call(
        functools.partial(layer_kernel, columns, count),
        out_shape=jax.ShapeDtypeStruct((rows, HDIM), bf16),
        in_specs=[hbm] * 8,
        out_specs=vmem,
        scratch_shapes=[
            pltpu.VMEM(contact_tiles.shape, bf16),
            pltpu.SMEM(tile_codes.shape, jnp.int32),
            pltpu.VMEM(valid.shape, jnp.int32),
            pltpu.VMEM(activations.shape, bf16),
            pltpu.VMEM(dilated_tap_weight.shape, bf16),
            pltpu.VMEM(conv_mix.shape, bf16),
            pltpu.VMEM(w_query.shape, bf16),
            pltpu.VMEM(w_keyval.shape, bf16),
            pltpu.VMEM((2, edge, channels), bf16),
            pltpu.VMEM((rows + 2 * edge, channels), bf16),
            pltpu.VMEM((half_rows, hidden), bf16),
            pltpu.VMEM((half_rows, channels), f32),
            pltpu.VMEM((half_rows, channels), bf16),
            pltpu.VMEM(contact_tiles.shape, f32),
            pltpu.VMEM((2 * HDIM, rows), bf16),
            pltpu.VMEM((rows, rows), f32),
            pltpu.VMEM((rows, rows), bf16),
            pltpu.VMEM((count, rows // tile, 2 * tile, HDIM), bf16),
            pltpu.VMEM((1, rows), f32),
            pltpu.VMEM((HDIM + 16, rows), f32),
            pltpu.SemaphoreType.DMA((11,)),
            pltpu.SemaphoreType.DMA((2,)),
            pltpu.SemaphoreType.DMA((2,)),
            pltpu.SemaphoreType.DMA((4, (2 * far + 1) * columns, 2)),
            pltpu.SemaphoreType.DMA((count, 2)),
        ],
        compiler_params=pltpu.CompilerParams(
            collective_id=0, has_side_effects=True, vmem_limit_bytes=56 * 1024 * 1024
        ),
        cost_estimate=pl.CostEstimate(
            flops=2 * rows * channels * (4 * hidden + 3 * HDIM) + 4 * rows * HDIM * 2 * HALF,
            bytes_accessed=14 * 1024 * 1024,
            transcendentals=rows * 2 * HALF,
        ),
    )(
        activations,
        dilated_tap_weight,
        conv_mix,
        w_query,
        w_keyval,
        contact_tiles,
        tile_codes,
        valid,
    )


def columns_of(mesh):
    along = mesh.devices.reshape(-1, mesh.shape["seq"])[0]
    first = along[0]
    if not hasattr(first, "coords"):
        return 2 if mesh.shape["seq"] == 16 else 1
    return sum(d.coords[2] == first.coords[2] for d in along) // 2


def solution(mesh):
    in_specs = (P(("grp", "seq"), None), P(), P(), P(), P(), P(), P(("grp", "seq"), None), P("grp"))
    out_specs = P(("grp", "seq"), None)
    return jax.shard_map(
        functools.partial(per_device, columns_of(mesh)),
        mesh=mesh,
        in_specs=in_specs,
        out_specs=out_specs,
        check_vma=False,
    )
```

```python
import functools
import math

import jax
import jax.numpy as jnp
from jax import lax
from jax.experimental import pallas as pl
from jax.experimental.pallas import tpu as pltpu
from jax.sharding import PartitionSpec as P

HDIM = 128
CONV_DILATION = 8
HALF = 4096
MESH = pl.DeviceIdType.MESH

masked_score = -1e30
norm_eps = 1e-06
LOG2E = math.log2(math.e)


class Place:
    def __init__(self, count, columns, reach):
        self.count = count
        self.columns = columns
        self.plane = 2 * columns
        self.planes = count // self.plane
        self.reach = reach
        self.far = -(-reach // self.plane)
        self.steps = (2 * self.far + 1) * columns
        me = lax.axis_index("seq")
        self.me = me
        self.z = me // self.plane
        self.y = (me % self.plane) // 2
        self.core = me % 2

    def index(self, z, y, core):
        return z * self.plane + y * 2 + core

    def order(self):
        blocks = [(0, 0)]
        late = [(0, 1)]
        for d in range(1, self.far + 1):
            if d == 1 and self.columns == 2:
                blocks += late
                late = []
            blocks += [(-d, 0), (d, 0)]
            if d > 1 and self.columns == 2:
                blocks += late
            late = [(-d, 1), (d, 1)]
        if self.columns == 2:
            blocks += late
        return blocks

    def hand_order(self):
        blocks = self.order()
        first = self.near()
        steps = [(0, k, 0) for k in range(1, first + 1)]
        steps += [(1, k, 1) for k in range(1, first + 1)]
        for k in range(first + 1, len(blocks), 2):
            turn, later = 2 * k - 4, 2 * k - 2
            if self.columns == 2 and k == first + 1:
                turn, later = 2, 6
            elif self.columns == 2 and k == first + 3:
                turn, later = 6, 8
            steps += [(turn, k, 0), (turn, k + 1, 0), (later, k, 1), (later, k + 1, 1)]
        return steps

    def near(self):
        return 3 if self.columns == 2 else 2

    def step(self, k):
        dz = flip = jnp.int32(0)
        for i, (d, f) in enumerate(self.order()):
            dz = jnp.where(k == i, d, dz)
            flip = jnp.where(k == i, f, flip)
        return dz, flip

    def needs(self, source, target):
        return jnp.abs(source - target) <= self.reach


def block_moves(place, kvbuf, send_sem, recv_sem, dz, flip, half, part):
    z, y, core = place.z, place.y, place.core
    source_z = z + dz
    source = place.index(source_z, (y + flip) % 2 if place.columns == 2 else y, core)
    held = (source_z >= 0) & (source_z < place.planes) & place.needs(source, place.me)
    piece = kvbuf.at[source, pl.ds(half * part, part)]
    slot = (dz + place.far) * place.columns + flip
    edge = (source_z == 0) | (source_z == place.planes - 1)
    away = jnp.abs(dz)

    def along_z(distance):
        return (distance == 1) & (edge | (half == 1))

    def copy(kind, target):
        return pltpu.make_async_remote_copy(
            src_ref=piece,
            dst_ref=piece,
            send_sem=send_sem.at[kind, slot, half],
            recv_sem=recv_sem.at[source, half],
            device_id={"seq": target},
            device_id_type=MESH,
        )

    moves = []
    for kind, turn in ((0, 1), (1, -1)):
        target = jnp.clip(place.index(z + turn, y, core), 0, place.count - 1)
        go = held & (z + turn >= 0) & (z + turn < place.planes)
        go = go & (dz * turn <= 0) & (away + 1 <= place.far) & place.needs(source, target)
        go = go & ((flip == 0) | along_z(away + 1))
        moves.append((go, copy(kind, target)))
    if place.columns == 2:
        target = place.index(z, 1 - y, core)
        go = held & (flip == 0) & ((dz == 0) | jnp.logical_not(along_z(away)))
        moves.append((go & place.needs(source, target), copy(2, target)))
    target = place.index(z, y, 1 - core)
    moves.append((held & place.needs(source, target), copy(3, target)))
    return source, held, moves


def gelu(v):
    size = jnp.abs(v)
    low = 1.0 + (0.3275911 * math.sqrt(0.5)) * size
    t = pl.reciprocal(low, approx=True)
    t = t * (2.0 - low * t)
    poly = 0.5 * 1.061405429 * t - 0.5 * 1.453152027
    poly = poly * t + 0.5 * 1.421413741
    poly = poly * t - 0.5 * 0.284496736
    poly = (poly * t + 0.5 * 0.254829592) * t
    tail = poly * jnp.exp2((-0.5 * LOG2E) * (size * size))
    return jnp.maximum(v, 0.0) - size * tail


def layer_kernel(
    columns,
    count,
    act_hbm,
    taps_hbm,
    mix_hbm,
    wq_hbm,
    wkv_hbm,
    tiles_hbm,
    codes_hbm,
    valid_hbm,
    out_ref,
    tiles_ref,
    codes_ref,
    valid_ref,
    act,
    taps,
    mix,
    wq,
    wkv,
    halo,
    lifted,
    squeezed,
    mixed,
    normed,
    table,
    queries,
    scores_buf,
    probs_buf,
    kvbuf,
    peak,
    weighted,
    load_sem,
    halo_send,
    halo_recv,
    send_sem,
    recv_sem,
):
    rows, channels = act.shape
    hidden = mix.shape[0]
    half_rows = rows // 2
    tile = table.shape[1]
    tiles = rows // tile
    offsets = codes_ref.shape[1]
    edge = halo.shape[1]
    early_rows = half_rows + 2 * edge
    place = Place(count, columns, HALF // rows)
    me, z, y, core = place.me, place.z, place.y, place.core

    wide = 256
    parts = hidden // wide
    loads = [
        pltpu.make_async_copy(
            act_hbm.at[pl.ds(0, early_rows)], act.at[pl.ds(0, early_rows)], load_sem.at[0]
        ),
        pltpu.make_async_copy(
            act_hbm.at[pl.ds(early_rows, rows - early_rows)],
            act.at[pl.ds(early_rows, rows - early_rows)],
            load_sem.at[1],
        ),
    ]
    tap_loads = [
        pltpu.make_async_copy(taps_hbm.at[tap], taps.at[tap], load_sem.at[5 + tap])
        for tap in range(3)
    ]
    late_loads = [
        pltpu.make_async_copy(mix_hbm, mix, load_sem.at[2]),
        pltpu.make_async_copy(wkv_hbm, wkv, load_sem.at[3]),
        pltpu.make_async_copy(wq_hbm, wq, load_sem.at[4]),
    ]
    small_loads = [
        pltpu.make_async_copy(tiles_hbm, tiles_ref, load_sem.at[8]),
        pltpu.make_async_copy(codes_hbm, codes_ref, load_sem.at[9]),
        pltpu.make_async_copy(valid_hbm, valid_ref, load_sem.at[10]),
    ]
    for load in loads + tap_loads + late_loads + small_loads:
        load.start()

    barrier = pltpu.get_barrier_semaphore()
    greeted = [(jnp.bool_(True), place.index(z, y, 1 - core))]
    if columns == 2:
        greeted.append((jnp.bool_(True), place.index(z, 1 - y, core)))
    for turn in (1, -1):
        ok = (z + turn >= 0) & (z + turn < place.planes)
        greeted.append((ok, jnp.clip(place.index(z + turn, y, core), 0, count - 1)))
    beyond = me + 2 * core - 1
    greeted.append(((beyond >= 0) & (beyond < count), jnp.clip(beyond, 0, count - 1)))
    for ok, target in greeted:

        @pl.when(ok)
        def _():
            pl.semaphore_signal(barrier, inc=1, device_id={"seq": target}, device_id_type=MESH)

    loads[0].wait()
    loads[1].wait()
    pl.semaphore_wait(barrier, sum(ok.astype(jnp.int32) for ok, _target in greeted))

    has_next = me + 1 < count
    has_prev = me > 0
    to_next = pltpu.make_async_remote_copy(
        src_ref=act.at[pl.ds(rows - edge, edge)],
        dst_ref=halo.at[0],
        send_sem=halo_send.at[0],
        recv_sem=halo_recv.at[0],
        device_id={"seq": jnp.minimum(me + 1, count - 1)},
        device_id_type=MESH,
    )
    to_prev = pltpu.make_async_remote_copy(
        src_ref=act.at[pl.ds(0, edge)],
        dst_ref=halo.at[1],
        send_sem=halo_send.at[1],
        recv_sem=halo_recv.at[1],
        device_id={"seq": jnp.maximum(me - 1, 0)},
        device_id_type=MESH,
    )

    @pl.when(has_next)
    def _():
        to_next.start()

    @pl.when(has_prev)
    def _():
        to_prev.start()

    peak[...] = jnp.full(peak.shape, masked_score, jnp.float32)
    spare = lax.broadcasted_iota(jnp.int32, (HDIM, rows), 0) == 0
    queries[HDIM:] = jnp.where(spare, 1.0, 0.0).astype(jnp.bfloat16)
    weighted[...] = jnp.zeros(weighted.shape, jnp.float32)

    def lift(at, count):
        raised = gelu(act[pl.ds(at, count)].astype(jnp.float32))
        lifted[pl.ds(at + edge, count)] = raised.astype(jnp.bfloat16)

    def lift_strip(strip, carry):
        lift(pl.multiple_of(strip * 2 * edge, 2 * edge), 2 * edge)
        return carry

    def turn_tile(code):
        table[code] = tiles_ref[code].T.astype(jnp.float32) * LOG2E

    lax.fori_loop(0, early_rows // (2 * edge), lift_strip, 0)

    def lift_halo(side, there, copy):
        at = side * (rows + edge)

        @pl.when(there)
        def _():
            copy.wait_recv()
            lifted[at : at + edge] = gelu(halo[side].astype(jnp.float32)).astype(jnp.bfloat16)

        @pl.when(jnp.logical_not(there))
        def _():
            lifted[at : at + edge] = jnp.zeros((edge, channels), jnp.bfloat16)

    lift_halo(0, has_prev, to_next)

    def moves_of(k, half):
        dz, flip = place.step(k)
        return block_moves(place, kvbuf, send_sem, recv_sem, dz, flip, half, tiles // 2)

    def hand_on(held, moves):
        for go, copy in moves:

            @pl.when(go & held)
            def _():
                copy.start()

    def arrived(source, half):
        piece = kvbuf.at[source, pl.ds(half * (tiles // 2), tiles // 2)]
        pltpu.make_async_copy(piece, piece, recv_sem.at[source, half]).wait()

    hand_steps = place.hand_order()

    def hand_one(c, carry):
        k = half = jnp.int32(0)
        for i, (_turn, block, part) in enumerate(hand_steps):
            k = jnp.where(c == i, block, k)
            half = jnp.where(c == i, part, half)
        source, held, moves = moves_of(k, half)

        @pl.when(held)
        def _():
            arrived(source, half)

        hand_on(held, moves)
        return carry

    shift = CONV_DILATION
    tall = half_rows + edge

    def convolve(half, beside):
        at = half * half_rows
        for p in range(parts):
            cols = slice(p * wide, (p + 1) * wide)
            low = jnp.dot(
                lifted[at : at + tall], taps[0, :, cols], preferred_element_type=jnp.float32
            )
            mid = jnp.dot(
                lifted[at + edge : at + edge + half_rows],
                taps[1, :, cols],
                preferred_element_type=jnp.float32,
            )
            high = jnp.dot(
                lifted[at + edge : at + edge + tall],
                taps[2, :, cols],
                preferred_element_type=jnp.float32,
            )
            for task in beside[p::parts]:
                task()
            conv = low[edge - shift : edge - shift + half_rows] + mid
            conv = conv + high[shift : shift + half_rows]
            squeezed[:, cols] = gelu(conv).astype(jnp.bfloat16)

    def project(half):
        at = half * half_rows
        here = slice(at, at + half_rows)
        square = jnp.zeros((half_rows, 128), jnp.float32)
        for n in range(0, channels, wide):
            part = act[here, n : n + wide].astype(jnp.float32) + jnp.dot(
                squeezed[...], mix[:, n : n + wide], preferred_element_type=jnp.float32
            )
            mixed[:, n : n + wide] = part
            for m in range(0, wide, 128):
                square = square + part[:, m : m + 128] * part[:, m : m + 128]
        mean = jnp.sum(square, axis=1, keepdims=True) * (1.0 / channels)
        factor = lax.rsqrt(mean + norm_eps)
        for n in range(0, channels, wide):
            normed[:, n : n + wide] = (mixed[:, n : n + wide] * factor).astype(jnp.bfloat16)
        keyval = jnp.dot(normed[...], wkv[...], preferred_element_type=jnp.float32)
        keys = keyval[:, :HDIM].astype(jnp.bfloat16)
        values = keyval[:, HDIM:].T.astype(jnp.bfloat16)
        for j in range(tiles // 2):
            cut = slice(j * tile, (j + 1) * tile)
            kvbuf[me, half * (tiles // 2) + j, :tile] = keys[cut]
            kvbuf[me, half * (tiles // 2) + j, tile:] = values[:, cut]
        _source, held, moves = moves_of(0, half)
        hand_on(held, moves)
        query = jnp.dot(normed[...], wq[...], preferred_element_type=jnp.float32)
        query = (query * (LOG2E / math.sqrt(HDIM))).T.astype(jnp.bfloat16)
        queries[:HDIM, here] = query

    beside = [functools.partial(lift, at, edge) for at in range(early_rows, rows, edge)]
    beside += [functools.partial(turn_tile, code) for code in range(tiles_ref.shape[0])]
    for load in tap_loads + small_loads[:1]:
        load.wait()
    convolve(0, beside)
    for load in late_loads:
        load.wait()
    project(0)
    lift_halo(1, has_next, to_prev)
    convolve(1, [])
    lax.fori_loop(0, place.near(), hand_one, 0)
    project(1)
    for load in small_loads[1:]:
        load.wait()

    def absorb(source, special):
        delta = source - me
        keys = jnp.concatenate([kvbuf[source, j, :tile] for j in range(tiles)], axis=0)
        values = jnp.concatenate([kvbuf[source, j, tile:] for j in range(tiles)], axis=1)
        values = jnp.concatenate([values, jnp.ones((16, rows), jnp.bfloat16)], axis=0)
        line = [valid_ref[pl.ds(source * tiles + j, 1)] for j in range(tiles)]
        line = jnp.where(jnp.concatenate(line, axis=1) == 1, 0.0, masked_score)
        line = jnp.broadcast_to(line, (16, rows)).astype(jnp.bfloat16)
        mask = lax.dot_general(
            line,
            jnp.ones((16, HDIM), jnp.bfloat16),
            (((0,), (0,)), ((), ())),
            preferred_element_type=jnp.float32,
        )
        if special:
            looked = queries.at[:HDIM]
        else:
            keys = jnp.concatenate([keys, mask.astype(jnp.bfloat16)], axis=1)
            looked = queries
        spans = [slice(n, n + 2 * tile) for n in range(0, rows, 2 * tile)]
        for span in spans:
            scores_buf[:, span] = jnp.dot(
                keys, looked[:, span], preferred_element_type=jnp.float32
            )
        for span in spans:
            shrinks = []
            for i in range(span.start // tile, span.stop // tile):
                across = slice(i * tile, (i + 1) * tile)
                column = []
                highs = []
                for j in range(tiles):
                    down = slice(j * tile, (j + 1) * tile)
                    offset = jnp.clip(delta * tiles + (j - i) + offsets // 2, 0, offsets - 1)
                    scores = scores_buf[down, across] + table[codes_ref[i, offset]]
                    if special and i == j:
                        key_row = lax.broadcasted_iota(jnp.int32, (tile, tile), 0)
                        query_row = lax.broadcasted_iota(jnp.int32, (tile, tile), 1)
                        apart = delta * rows + key_row - query_row
                        kept = (apart == 0) | ((jnp.abs(apart) <= HALF) & (mask[down] >= 0.0))
                        scores = jnp.where(kept, scores, masked_score)
                    elif special:
                        away = jnp.abs(delta * tiles + (j - i))
                        scores = scores + mask[down]
                        scores = scores + jnp.where(away <= HALF // tile, 0.0, masked_score)
                    column.append(scores)
                    highs.append(jnp.max(scores.reshape(tile // 8, 8, tile), axis=0))
                while len(highs) > 1:
                    highs = [jnp.maximum(u, v) for u, v in zip(highs[::2], highs[1::2])]
                old = peak[:, across]
                new = jnp.maximum(old, jnp.max(highs[0], axis=0, keepdims=True))
                for j in range(tiles):
                    probs_buf[j * tile : (j + 1) * tile, across] = jnp.exp2(
                        column[j] - new
                    ).astype(jnp.bfloat16)
                peak[:, across] = new
                shrinks.append(jnp.exp2(old - new))
            shrink = jnp.concatenate(shrinks, axis=1)
            weighted[:, span] = weighted[:, span] * shrink + jnp.dot(
                values, probs_buf[:, span], preferred_element_type=jnp.float32
            )

    def absorb_block(source):
        apart = jnp.abs(source - me)
        special = (apart == 0) | (apart == place.reach)

        @pl.when(special)
        def _():
            absorb(source, True)

        @pl.when(jnp.logical_not(special))
        def _():
            absorb(source, False)

    turns = 2 * place.steps

    def hand_one(c, carry):
        k = half = jnp.int32(0)
        for i, (_turn, block, part) in enumerate(hand_steps):
            k = jnp.where(c == i, block, k)
            half = jnp.where(c == i, part, half)
        source, held, moves = moves_of(k, half)

        @pl.when(held)
        def _():
            arrived(source, half)

        hand_on(held, moves)
        return carry

    def turn_of(u, done):
        until = jnp.int32(0)
        for turn, _block, _part in hand_steps:
            until = until + jnp.where(turn <= u, 1, 0)
        lax.fori_loop(done, until, hand_one, 0)
        dz, flip = place.step(u // 2)
        away = u % 2
        source_z = z + dz
        column = (y + flip) % 2 if columns == 2 else y
        source = place.index(source_z, column, (core + away) % 2)
        take = (source_z >= 0) & (source_z < place.planes) & place.needs(source, me)

        @pl.when(take)
        def _():
            @pl.when(away == 1)
            def _():
                arrived(source, 0)
                arrived(source, 1)

            absorb_block(source)

        return until

    lax.fori_loop(0, turns, turn_of, jnp.int32(place.near()))
    result = weighted[:HDIM] / weighted[HDIM : HDIM + 1]
    out_ref[...] = result.T.astype(out_ref.dtype)

    def drain(k, carry):
        for half in range(2):
            _source, _held, moves = moves_of(k, half)
            for go, copy in moves:

                @pl.when(go)
                def _():
                    copy.wait_send()

        return carry

    lax.fori_loop(0, place.steps, drain, 0)

    @pl.when(has_next)
    def _():
        to_next.wait_send()

    @pl.when(has_prev)
    def _():
        to_prev.wait_send()


def per_device(
    columns,
    activations,
    dilated_tap_weight,
    conv_mix,
    w_query,
    w_keyval,
    contact_tiles,
    tile_codes,
    bin_valid,
):
    rows, channels = activations.shape
    hidden = conv_mix.shape[0]
    half_rows = rows // 2
    edge = 16
    tile = contact_tiles.shape[1]
    count = lax.axis_size("seq")
    plane = 2 * columns
    far = -(-(HALF // rows) // plane)
    valid = bin_valid.reshape(count * rows // tile, tile)
    vmem = pl.BlockSpec(memory_space=pltpu.VMEM)
    hbm = pl.BlockSpec(memory_space=pl.ANY)
    bf16, f32 = jnp.bfloat16, jnp.float32
    return pl.pallas_call(
        functools.partial(layer_kernel, columns, count),
        out_shape=jax.ShapeDtypeStruct((rows, HDIM), bf16),
        in_specs=[hbm] * 8,
        out_specs=vmem,
        scratch_shapes=[
            pltpu.VMEM(contact_tiles.shape, bf16),
            pltpu.SMEM(tile_codes.shape, jnp.int32),
            pltpu.VMEM(valid.shape, jnp.int32),
            pltpu.VMEM(activations.shape, bf16),
            pltpu.VMEM(dilated_tap_weight.shape, bf16),
            pltpu.VMEM(conv_mix.shape, bf16),
            pltpu.VMEM(w_query.shape, bf16),
            pltpu.VMEM(w_keyval.shape, bf16),
            pltpu.VMEM((2, edge, channels), bf16),
            pltpu.VMEM((rows + 2 * edge, channels), bf16),
            pltpu.VMEM((half_rows, hidden), bf16),
            pltpu.VMEM((half_rows, channels), f32),
            pltpu.VMEM((half_rows, channels), bf16),
            pltpu.VMEM(contact_tiles.shape, f32),
            pltpu.VMEM((2 * HDIM, rows), bf16),
            pltpu.VMEM((rows, rows), f32),
            pltpu.VMEM((rows, rows), bf16),
            pltpu.VMEM((count, rows // tile, 2 * tile, HDIM), bf16),
            pltpu.VMEM((1, rows), f32),
            pltpu.VMEM((HDIM + 16, rows), f32),
            pltpu.SemaphoreType.DMA((11,)),
            pltpu.SemaphoreType.DMA((2,)),
            pltpu.SemaphoreType.DMA((2,)),
            pltpu.SemaphoreType.DMA((4, (2 * far + 1) * columns, 2)),
            pltpu.SemaphoreType.DMA((count, 2)),
        ],
        compiler_params=pltpu.CompilerParams(
            collective_id=0, has_side_effects=True, vmem_limit_bytes=56 * 1024 * 1024
        ),
        cost_estimate=pl.CostEstimate(
            flops=2 * rows * channels * (4 * hidden + 3 * HDIM) + 4 * rows * HDIM * 2 * HALF,
            bytes_accessed=14 * 1024 * 1024,
            transcendentals=rows * 2 * HALF,
        ),
    )(
        activations,
        dilated_tap_weight,
        conv_mix,
        w_query,
        w_keyval,
        contact_tiles,
        tile_codes,
        valid,
    )


def columns_of(mesh):
    along = mesh.devices.reshape(-1, mesh.shape["seq"])[0]
    first = along[0]
    if not hasattr(first, "coords"):
        return 2 if mesh.shape["seq"] == 16 else 1
    return sum(d.coords[2] == first.coords[2] for d in along) // 2


def solution(mesh):
    in_specs = (P(("grp", "seq"), None), P(), P(), P(), P(), P(), P(("grp", "seq"), None), P("grp"))
    out_specs = P(("grp", "seq"), None)
    return jax.shard_map(
        functools.partial(per_device, columns_of(mesh)),
        mesh=mesh,
        in_specs=in_specs,
        out_specs=out_specs,
        check_vma=False,
    )
```

```python
import functools
import math

import jax
import jax.numpy as jnp
from jax import lax
from jax.experimental import pallas as pl
from jax.experimental.pallas import tpu as pltpu
from jax.sharding import PartitionSpec as P

HDIM = 128
CONV_DILATION = 8
HALF = 4096
MESH = pl.DeviceIdType.MESH

masked_score = -1e30
norm_eps = 1e-06
LOG2E = math.log2(math.e)


class Place:
    def __init__(self, count, columns, reach):
        self.count = count
        self.columns = columns
        self.plane = 2 * columns
        self.planes = count // self.plane
        self.reach = reach
        self.far = -(-reach // self.plane)
        self.steps = (2 * self.far + 1) * columns
        me = lax.axis_index("seq")
        self.me = me
        self.z = me // self.plane
        self.y = (me % self.plane) // 2
        self.core = me % 2

    def index(self, z, y, core):
        return z * self.plane + y * 2 + core

    def order(self):
        blocks = [(0, 0)]
        late = [(0, 1)]
        for d in range(1, self.far + 1):
            if d == 1 and self.columns == 2:
                blocks += late
                late = []
            blocks += [(-d, 0), (d, 0)]
            if d > 1 and self.columns == 2:
                blocks += late
            late = [(-d, 1), (d, 1)]
        if self.columns == 2:
            blocks += late
        return blocks

    def hand_order(self):
        blocks = self.order()
        first = self.near()
        steps = [(0, k, 0) for k in range(1, first + 1)]
        steps += [(1, k, 1) for k in range(1, first + 1)]
        for k in range(first + 1, len(blocks), 2):
            turn, later = 2 * k - 4, 2 * k - 2
            if self.columns == 2 and k == first + 1:
                turn, later = 2, 6
            elif self.columns == 2 and k == first + 3:
                turn, later = 6, 8
            steps += [(turn, k, 0), (turn, k + 1, 0), (later, k, 1), (later, k + 1, 1)]
        return steps

    def near(self):
        return 3 if self.columns == 2 else 2

    def step(self, k):
        dz = flip = jnp.int32(0)
        for i, (d, f) in enumerate(self.order()):
            dz = jnp.where(k == i, d, dz)
            flip = jnp.where(k == i, f, flip)
        return dz, flip

    def needs(self, source, target):
        return jnp.abs(source - target) <= self.reach


def block_moves(place, kvbuf, send_sem, recv_sem, dz, flip, half, part):
    z, y, core = place.z, place.y, place.core
    source_z = z + dz
    source = place.index(source_z, (y + flip) % 2 if place.columns == 2 else y, core)
    held = (source_z >= 0) & (source_z < place.planes) & place.needs(source, place.me)
    piece = kvbuf.at[source, pl.ds(half * part, part)]
    slot = (dz + place.far) * place.columns + flip
    edge = (source_z == 0) | (source_z == place.planes - 1)
    away = jnp.abs(dz)

    def along_z(distance):
        return (distance == 1) & (edge | (half == 1))

    def copy(kind, target):
        return pltpu.make_async_remote_copy(
            src_ref=piece,
            dst_ref=piece,
            send_sem=send_sem.at[kind, slot, half],
            recv_sem=recv_sem.at[source, half],
            device_id={"seq": target},
            device_id_type=MESH,
        )

    moves = []
    for kind, turn in ((0, 1), (1, -1)):
        target = jnp.clip(place.index(z + turn, y, core), 0, place.count - 1)
        go = held & (z + turn >= 0) & (z + turn < place.planes)
        go = go & (dz * turn <= 0) & (away + 1 <= place.far) & place.needs(source, target)
        go = go & ((flip == 0) | along_z(away + 1))
        moves.append((go, copy(kind, target)))
    if place.columns == 2:
        target = place.index(z, 1 - y, core)
        go = held & (flip == 0) & ((dz == 0) | jnp.logical_not(along_z(away)))
        moves.append((go & place.needs(source, target), copy(2, target)))
    target = place.index(z, y, 1 - core)
    moves.append((held & place.needs(source, target), copy(3, target)))
    return source, held, moves


def gelu(v):
    size = jnp.abs(v)
    low = 1.0 + (0.3275911 * math.sqrt(0.5)) * size
    t = pl.reciprocal(low, approx=True)
    t = t * (2.0 - low * t)
    poly = 0.5 * 1.061405429 * t - 0.5 * 1.453152027
    poly = poly * t + 0.5 * 1.421413741
    poly = poly * t - 0.5 * 0.284496736
    poly = (poly * t + 0.5 * 0.254829592) * t
    tail = poly * jnp.exp2((-0.5 * LOG2E) * (size * size))
    return jnp.maximum(v, 0.0) - size * tail


def layer_kernel(
    columns,
    count,
    act_hbm,
    taps_hbm,
    mix_hbm,
    wq_hbm,
    wkv_hbm,
    tiles_hbm,
    codes_hbm,
    valid_hbm,
    out_ref,
    tiles_ref,
    codes_ref,
    valid_ref,
    act,
    taps,
    mix,
    wq,
    wkv,
    halo,
    lifted,
    squeezed,
    mixed,
    normed,
    table,
    queries,
    scores_buf,
    probs_buf,
    kvbuf,
    peak,
    weighted,
    load_sem,
    halo_send,
    halo_recv,
    send_sem,
    recv_sem,
):
    rows, channels = act.shape
    hidden = mix.shape[0]
    half_rows = rows // 2
    tile = table.shape[1]
    tiles = rows // tile
    offsets = codes_ref.shape[1]
    edge = halo.shape[1]
    early_rows = half_rows + 2 * edge
    place = Place(count, columns, HALF // rows)
    me, z, y, core = place.me, place.z, place.y, place.core

    wide = 256
    parts = hidden // wide
    loads = [
        pltpu.make_async_copy(
            act_hbm.at[pl.ds(0, early_rows)], act.at[pl.ds(0, early_rows)], load_sem.at[0]
        ),
        pltpu.make_async_copy(
            act_hbm.at[pl.ds(early_rows, rows - early_rows)],
            act.at[pl.ds(early_rows, rows - early_rows)],
            load_sem.at[1],
        ),
    ]
    tap_loads = [
        pltpu.make_async_copy(taps_hbm.at[tap], taps.at[tap], load_sem.at[5 + tap])
        for tap in range(3)
    ]
    late_loads = [
        pltpu.make_async_copy(mix_hbm, mix, load_sem.at[2]),
        pltpu.make_async_copy(wkv_hbm, wkv, load_sem.at[3]),
        pltpu.make_async_copy(wq_hbm, wq, load_sem.at[4]),
    ]
    small_loads = [
        pltpu.make_async_copy(tiles_hbm, tiles_ref, load_sem.at[8]),
        pltpu.make_async_copy(codes_hbm, codes_ref, load_sem.at[9]),
        pltpu.make_async_copy(valid_hbm, valid_ref, load_sem.at[10]),
    ]
    for load in loads + tap_loads + late_loads + small_loads:
        load.start()

    barrier = pltpu.get_barrier_semaphore()
    greeted = [(jnp.bool_(True), place.index(z, y, 1 - core))]
    if columns == 2:
        greeted.append((jnp.bool_(True), place.index(z, 1 - y, core)))
    for turn in (1, -1):
        ok = (z + turn >= 0) & (z + turn < place.planes)
        greeted.append((ok, jnp.clip(place.index(z + turn, y, core), 0, count - 1)))
    beyond = me + 2 * core - 1
    greeted.append(((beyond >= 0) & (beyond < count), jnp.clip(beyond, 0, count - 1)))
    for ok, target in greeted:

        @pl.when(ok)
        def _():
            pl.semaphore_signal(barrier, inc=1, device_id={"seq": target}, device_id_type=MESH)

    loads[0].wait()
    loads[1].wait()
    pl.semaphore_wait(barrier, sum(ok.astype(jnp.int32) for ok, _target in greeted))

    has_next = me + 1 < count
    has_prev = me > 0
    to_next = pltpu.make_async_remote_copy(
        src_ref=act.at[pl.ds(rows - edge, edge)],
        dst_ref=halo.at[0],
        send_sem=halo_send.at[0],
        recv_sem=halo_recv.at[0],
        device_id={"seq": jnp.minimum(me + 1, count - 1)},
        device_id_type=MESH,
    )
    to_prev = pltpu.make_async_remote_copy(
        src_ref=act.at[pl.ds(0, edge)],
        dst_ref=halo.at[1],
        send_sem=halo_send.at[1],
        recv_sem=halo_recv.at[1],
        device_id={"seq": jnp.maximum(me - 1, 0)},
        device_id_type=MESH,
    )

    @pl.when(has_next)
    def _():
        to_next.start()

    @pl.when(has_prev)
    def _():
        to_prev.start()

    peak[...] = jnp.full(peak.shape, masked_score, jnp.float32)
    spare = lax.broadcasted_iota(jnp.int32, (HDIM, rows), 0) == 0
    queries[HDIM:] = jnp.where(spare, 1.0, 0.0).astype(jnp.bfloat16)
    weighted[...] = jnp.zeros(weighted.shape, jnp.float32)

    def lift(at, count):
        raised = gelu(act[pl.ds(at, count)].astype(jnp.float32))
        lifted[pl.ds(at + edge, count)] = raised.astype(jnp.bfloat16)

    def lift_strip(strip, carry):
        lift(pl.multiple_of(strip * 2 * edge, 2 * edge), 2 * edge)
        return carry

    def turn_tile(code):
        table[code] = tiles_ref[code].T.astype(jnp.float32) * LOG2E

    lax.fori_loop(0, early_rows // (2 * edge), lift_strip, 0)

    def lift_halo(side, there, copy):
        at = side * (rows + edge)

        @pl.when(there)
        def _():
            copy.wait_recv()
            lifted[at : at + edge] = gelu(halo[side].astype(jnp.float32)).astype(jnp.bfloat16)

        @pl.when(jnp.logical_not(there))
        def _():
            lifted[at : at + edge] = jnp.zeros((edge, channels), jnp.bfloat16)

    lift_halo(0, has_prev, to_next)

    def moves_of(k, half):
        dz, flip = place.step(k)
        return block_moves(place, kvbuf, send_sem, recv_sem, dz, flip, half, tiles // 2)

    def hand_on(held, moves):
        for go, copy in moves:

            @pl.when(go & held)
            def _():
                copy.start()

    def arrived(source, half):
        piece = kvbuf.at[source, pl.ds(half * (tiles // 2), tiles // 2)]
        pltpu.make_async_copy(piece, piece, recv_sem.at[source, half]).wait()

    hand_steps = place.hand_order()

    def hand_one(c, carry):
        k = half = jnp.int32(0)
        for i, (_turn, block, part) in enumerate(hand_steps):
            k = jnp.where(c == i, block, k)
            half = jnp.where(c == i, part, half)
        source, held, moves = moves_of(k, half)

        @pl.when(held)
        def _():
            arrived(source, half)

        hand_on(held, moves)
        return carry

    shift = CONV_DILATION
    tall = half_rows + edge

    def convolve(half, beside):
        at = half * half_rows
        for p in range(parts):
            cols = slice(p * wide, (p + 1) * wide)
            low = jnp.dot(
                lifted[at : at + tall], taps[0, :, cols], preferred_element_type=jnp.float32
            )
            mid = jnp.dot(
                lifted[at + edge : at + edge + half_rows],
                taps[1, :, cols],
                preferred_element_type=jnp.float32,
            )
            high = jnp.dot(
                lifted[at + edge : at + edge + tall],
                taps[2, :, cols],
                preferred_element_type=jnp.float32,
            )
            for task in beside[p::parts]:
                task()
            conv = low[edge - shift : edge - shift + half_rows] + mid
            conv = conv + high[shift : shift + half_rows]
            squeezed[:, cols] = gelu(conv).astype(jnp.bfloat16)

    def project(half):
        at = half * half_rows
        here = slice(at, at + half_rows)
        square = jnp.zeros((half_rows, 128), jnp.float32)
        for n in range(0, channels, wide):
            part = act[here, n : n + wide].astype(jnp.float32) + jnp.dot(
                squeezed[...], mix[:, n : n + wide], preferred_element_type=jnp.float32
            )
            mixed[:, n : n + wide] = part
            for m in range(0, wide, 128):
                square = square + part[:, m : m + 128] * part[:, m : m + 128]
        mean = jnp.sum(square, axis=1, keepdims=True) * (1.0 / channels)
        factor = lax.rsqrt(mean + norm_eps)
        for n in range(0, channels, wide):
            normed[:, n : n + wide] = (mixed[:, n : n + wide] * factor).astype(jnp.bfloat16)
        keyval = jnp.dot(normed[...], wkv[...], preferred_element_type=jnp.float32)
        keys = keyval[:, :HDIM].astype(jnp.bfloat16)
        values = keyval[:, HDIM:].T.astype(jnp.bfloat16)
        for j in range(tiles // 2):
            cut = slice(j * tile, (j + 1) * tile)
            kvbuf[me, half * (tiles // 2) + j, :tile] = keys[cut]
            kvbuf[me, half * (tiles // 2) + j, tile:] = values[:, cut]
        _source, held, moves = moves_of(0, half)
        hand_on(held, moves)
        query = jnp.dot(normed[...], wq[...], preferred_element_type=jnp.float32)
        query = (query * (LOG2E / math.sqrt(HDIM))).T.astype(jnp.bfloat16)
        queries[:HDIM, here] = query

    beside = [functools.partial(lift, at, edge) for at in range(early_rows, rows, edge)]
    beside += [functools.partial(turn_tile, code) for code in range(tiles_ref.shape[0])]
    for load in tap_loads + small_loads[:1]:
        load.wait()
    convolve(0, beside)
    for load in late_loads:
        load.wait()
    project(0)
    lift_halo(1, has_next, to_prev)
    convolve(1, [])
    lax.fori_loop(0, place.near(), hand_one, 0)
    project(1)
    for load in small_loads[1:]:
        load.wait()

    def absorb(source, special):
        delta = source - me
        keys = jnp.concatenate([kvbuf[source, j, :tile] for j in range(tiles)], axis=0)
        values = jnp.concatenate([kvbuf[source, j, tile:] for j in range(tiles)], axis=1)
        values = jnp.concatenate([values, jnp.ones((16, rows), jnp.bfloat16)], axis=0)
        line = [valid_ref[pl.ds(source * tiles + j, 1)] for j in range(tiles)]
        line = jnp.where(jnp.concatenate(line, axis=1) == 1, 0.0, masked_score)
        line = jnp.broadcast_to(line, (16, rows)).astype(jnp.bfloat16)
        mask = lax.dot_general(
            line,
            jnp.ones((16, HDIM), jnp.bfloat16),
            (((0,), (0,)), ((), ())),
            preferred_element_type=jnp.float32,
        )
        if special:
            looked = queries.at[:HDIM]
        else:
            keys = jnp.concatenate([keys, mask.astype(jnp.bfloat16)], axis=1)
            looked = queries
        spans = [slice(n, n + 2 * tile) for n in range(0, rows, 2 * tile)]
        for span in spans:
            scores_buf[:, span] = jnp.dot(
                keys, looked[:, span], preferred_element_type=jnp.float32
            )
        for span in spans:
            shrinks = []
            for i in range(span.start // tile, span.stop // tile):
                across = slice(i * tile, (i + 1) * tile)
                column = []
                highs = []
                for j in range(tiles):
                    down = slice(j * tile, (j + 1) * tile)
                    offset = jnp.clip(delta * tiles + (j - i) + offsets // 2, 0, offsets - 1)
                    scores = scores_buf[down, across] + table[codes_ref[i, offset]]
                    if special and i == j:
                        key_row = lax.broadcasted_iota(jnp.int32, (tile, tile), 0)
                        query_row = lax.broadcasted_iota(jnp.int32, (tile, tile), 1)
                        apart = delta * rows + key_row - query_row
                        kept = (apart == 0) | ((jnp.abs(apart) <= HALF) & (mask[down] >= 0.0))
                        scores = jnp.where(kept, scores, masked_score)
                    elif special:
                        away = jnp.abs(delta * tiles + (j - i))
                        scores = scores + mask[down]
                        scores = scores + jnp.where(away <= HALF // tile, 0.0, masked_score)
                    column.append(scores)
                    highs.append(jnp.max(scores.reshape(tile // 8, 8, tile), axis=0))
                while len(highs) > 1:
                    highs = [jnp.maximum(u, v) for u, v in zip(highs[::2], highs[1::2])]
                old = peak[:, across]
                new = jnp.maximum(old, jnp.max(highs[0], axis=0, keepdims=True))
                for j in range(tiles):
                    probs_buf[j * tile : (j + 1) * tile, across] = jnp.exp2(
                        column[j] - new
                    ).astype(jnp.bfloat16)
                peak[:, across] = new
                shrinks.append(jnp.exp2(old - new))
            shrink = jnp.concatenate(shrinks, axis=1)
            weighted[:, span] = weighted[:, span] * shrink + jnp.dot(
                values, probs_buf[:, span], preferred_element_type=jnp.float32
            )

    def absorb_block(source):
        apart = jnp.abs(source - me)
        special = (apart == 0) | (apart == place.reach)

        @pl.when(special)
        def _():
            absorb(source, True)

        @pl.when(jnp.logical_not(special))
        def _():
            absorb(source, False)

    turns = 2 * place.steps

    def hand_one(c, carry):
        k = half = jnp.int32(0)
        for i, (_turn, block, part) in enumerate(hand_steps):
            k = jnp.where(c == i, block, k)
            half = jnp.where(c == i, part, half)
        source, held, moves = moves_of(k, half)

        @pl.when(held)
        def _():
            arrived(source, half)

        hand_on(held, moves)
        return carry

    def turn_of(u, done):
        until = jnp.int32(0)
        for turn, _block, _part in hand_steps:
            until = until + jnp.where(turn <= u, 1, 0)
        lax.fori_loop(done, until, hand_one, 0)
        dz, flip = place.step(u // 2)
        away = u % 2
        source_z = z + dz
        column = (y + flip) % 2 if columns == 2 else y
        source = place.index(source_z, column, (core + away) % 2)
        take = (source_z >= 0) & (source_z < place.planes) & place.needs(source, me)

        @pl.when(take)
        def _():
            @pl.when(away == 1)
            def _():
                arrived(source, 0)
                arrived(source, 1)

            absorb_block(source)

        return until

    lax.fori_loop(0, turns, turn_of, jnp.int32(place.near()))
    result = weighted[:HDIM] / weighted[HDIM : HDIM + 1]
    out_ref[...] = result.T.astype(out_ref.dtype)

    def drain(k, carry):
        for half in range(2):
            _source, _held, moves = moves_of(k, half)
            for go, copy in moves:

                @pl.when(go)
                def _():
                    copy.wait_send()

        return carry

    lax.fori_loop(0, place.steps, drain, 0)

    @pl.when(has_next)
    def _():
        to_next.wait_send()

    @pl.when(has_prev)
    def _():
        to_prev.wait_send()


def per_device(
    columns,
    activations,
    dilated_tap_weight,
    conv_mix,
    w_query,
    w_keyval,
    contact_tiles,
    tile_codes,
    bin_valid,
):
    rows, channels = activations.shape
    hidden = conv_mix.shape[0]
    half_rows = rows // 2
    edge = 16
    tile = contact_tiles.shape[1]
    count = lax.axis_size("seq")
    plane = 2 * columns
    far = -(-(HALF // rows) // plane)
    valid = bin_valid.reshape(count * rows // tile, tile)
    vmem = pl.BlockSpec(memory_space=pltpu.VMEM)
    hbm = pl.BlockSpec(memory_space=pl.ANY)
    bf16, f32 = jnp.bfloat16, jnp.float32
    return pl.pallas_call(
        functools.partial(layer_kernel, columns, count),
        out_shape=jax.ShapeDtypeStruct((rows, HDIM), bf16),
        in_specs=[hbm] * 8,
        out_specs=vmem,
        scratch_shapes=[
            pltpu.VMEM(contact_tiles.shape, bf16),
            pltpu.SMEM(tile_codes.shape, jnp.int32),
            pltpu.VMEM(valid.shape, jnp.int32),
            pltpu.VMEM(activations.shape, bf16),
            pltpu.VMEM(dilated_tap_weight.shape, bf16),
            pltpu.VMEM(conv_mix.shape, bf16),
            pltpu.VMEM(w_query.shape, bf16),
            pltpu.VMEM(w_keyval.shape, bf16),
            pltpu.VMEM((2, edge, channels), bf16),
            pltpu.VMEM((rows + 2 * edge, channels), bf16),
            pltpu.VMEM((half_rows, hidden), bf16),
            pltpu.VMEM((half_rows, channels), f32),
            pltpu.VMEM((half_rows, channels), bf16),
            pltpu.VMEM(contact_tiles.shape, f32),
            pltpu.VMEM((2 * HDIM, rows), bf16),
            pltpu.VMEM((rows, rows), f32),
            pltpu.VMEM((rows, rows), bf16),
            pltpu.VMEM((count, rows // tile, 2 * tile, HDIM), bf16),
            pltpu.VMEM((1, rows), f32),
            pltpu.VMEM((HDIM + 16, rows), f32),
            pltpu.SemaphoreType.DMA((11,)),
            pltpu.SemaphoreType.DMA((2,)),
            pltpu.SemaphoreType.DMA((2,)),
            pltpu.SemaphoreType.DMA((4, (2 * far + 1) * columns, 2)),
            pltpu.SemaphoreType.DMA((count, 2)),
        ],
        compiler_params=pltpu.CompilerParams(
            collective_id=0, has_side_effects=True, vmem_limit_bytes=55040 * 1024
        ),
        cost_estimate=pl.CostEstimate(
            flops=2 * rows * channels * (4 * hidden + 3 * HDIM) + 4 * rows * HDIM * 2 * HALF,
            bytes_accessed=14 * 1024 * 1024,
            transcendentals=rows * 2 * HALF,
        ),
    )(
        activations,
        dilated_tap_weight,
        conv_mix,
        w_query,
        w_keyval,
        contact_tiles,
        tile_codes,
        valid,
    )


def columns_of(mesh):
    along = mesh.devices.reshape(-1, mesh.shape["seq"])[0]
    first = along[0]
    if not hasattr(first, "coords"):
        return 2 if mesh.shape["seq"] == 16 else 1
    return sum(d.coords[2] == first.coords[2] for d in along) // 2


def solution(mesh):
    in_specs = (P(("grp", "seq"), None), P(), P(), P(), P(), P(), P(("grp", "seq"), None), P("grp"))
    out_specs = P(("grp", "seq"), None)
    return jax.shard_map(
        functools.partial(per_device, columns_of(mesh)),
        mesh=mesh,
        in_specs=in_specs,
        out_specs=out_specs,
        check_vma=False,
    )
```
